512 devices in a mesh: lat: 8 (over z_lo), lon: 64 (over y, x, z_hi, core).
Axes of the slice: x: 4, y: 4, z: 16 (z_hi: 2, z_lo: 8; z = z_hi * 8 + z_lo), core: 2. Of those that a mesh axis runs over, the one named last changes fastest.
Arguments:
- anomalies: bfloat16 [16, 256, 16, 256], P('lat', 'lon'), may hold values from -6 to 6
- background_mean: float32 [16, 256, 16], P('lat', 'lon'), may hold values from -6 to 6
- obs_anom: bfloat16 [8, 32768, 256], P('lat', 'lon'), may hold values from -4 to 4
- innovation: bfloat16 [8, 32768], P('lat', 'lon'), may hold values from -6 to 6
- obs_precision: bfloat16 [8, 32768], P('lat', 'lon'), may hold values from 0.5 to 4
- obs_blocks: int32 [8, 64], P('lat', 'lon'), may hold values from 1 to 4
- localization: float32 [8, 64, 7680], P('lat', 'lon'), may hold values from 0.15 to 1
- loc_pattern: int32 [8, 64, 60], P('lat', 'lon'), may hold values 0 or 1
Outputs:
- analysis: bfloat16 [16, 256, 16, 256], P('lat', 'lon')
The draws below stay inside these ranges and needn't reach their ends.
All inputs are finite; a program needn't handle non-finite values. Where the reference program divides by a largest or mean magnitude, that divisor is 1e-20 or more. No bound on the sum of `loc_pattern` on one device may be relied on, other than what follows from the above.
Results may differ from the reference program's by a relative error of at most 0.0075.
Values may be sent and summed in bfloat16 or wider, within the bound.
No kernel may reach another device: no remote copies, remote signals or barrier semaphores. Data moves between devices by JAX's collectives and lax.ppermute only.
A program may use at most 64 MiB of HBM per device.

```python
import math
import jax
import jax.numpy as jnp
import numpy as np
from jax import lax

K = 256
LEV = 16
G = 1
OBS_BLK = 4
LAT_REACH = 1
LON_REACH = 2
NSI = 5
OBS_DEV = 512
NEAR = 15
LATC = 16
LONC = 256
LAT_TILES = 8
LON_TILES = 64
N_LAT = 8
N_LON = 64


common_rank = 8


def common_rows(key):
    return jax.random.normal(key, (LAT_TILES, LON_TILES * OBS_DEV, common_rank), jnp.float32)


def draw_obs_anom(key, part):
    coeffs = common_rows(key)
    key = jax.random.fold_in(key, 11)
    direction_key, noise_key = jax.random.split(key)
    directions = jax.random.normal(direction_key, (common_rank, K), jnp.float32)
    shape = (LAT_TILES, LON_TILES * OBS_DEV, K)
    noise = jax.random.normal(noise_key, shape, jnp.float32) * 0.55
    strength = 0.16
    coherent = jnp.zeros(shape, jnp.float32)
    for index in range(common_rank):
        coherent = coherent + coeffs[:, :, index:index + 1] * directions[index][None, None, :]
    values = noise + strength / math.sqrt(common_rank) * coherent
    return jnp.clip(values, -4.0, 4.0).astype(jnp.bfloat16)


def draw_innovation(key, part):
    coeffs = common_rows(key)
    key = jax.random.fold_in(key, 23)
    mixing_key, noise_key = jax.random.split(key)
    mixing = jax.random.normal(mixing_key, (common_rank,), jnp.float32)
    shape = (LAT_TILES, LON_TILES * OBS_DEV)
    noise = jax.random.normal(noise_key, shape, jnp.float32) * 0.6
    strength = 0.8
    coherent = jnp.zeros(shape, jnp.float32)
    for index in range(common_rank):
        coherent = coherent + coeffs[:, :, index] * mixing[index]
    values = noise + strength / math.sqrt(common_rank) * coherent
    return jnp.clip(values, -6.0, 6.0).astype(jnp.bfloat16)


def with_ends(array, key, least, top_value):
    dims = array.shape
    spot = [jax.random.randint(jax.random.fold_in(key, axis), (), 0, dims[axis]) for axis in range(len(dims))]
    array = array.at[tuple(spot)].set(least)
    longest = dims.index(max(dims))
    spot[longest] = (spot[longest] + 1) % dims[longest]
    return array.at[tuple(spot)].set(top_value)


def level_of(own_key, extent, cuts, smallest, top_value):
    gain, own = 1.0, jax.random.fold_in(own_key, 6)
    for dim, parts in cuts:
        steps = jnp.exp(jax.random.uniform(jax.random.fold_in(own, dim), (parts,), jnp.float32, smallest / len(cuts), top_value / len(cuts)))
        gain = gain * jnp.repeat(steps, extent[dim] // parts).reshape([-1 if axis == dim else 1 for axis in range(len(extent))])
    return gain


def gaussian(key, dims, scale, most, shards=(), kind=jnp.bfloat16):
    array = scale * jax.random.normal(key, dims, jnp.float32)
    if shards:
        array = array * level_of(key, dims, shards, -0.22, 0.18)
    return jnp.clip(array, -most, most).astype(kind)


def setup_inputs(seed: int = 0) -> dict:
    keys = jax.random.split(jax.random.key(seed), 9)
    return {
        "anomalies": gaussian(keys[0], (LATC, LONC, LEV, K), 1.0, 6.0, ((0, 8), (1, 64))),
        "background_mean": gaussian(keys[1], (LATC, LONC, LEV), 1.0, 6.0, ((0, 8), (1, 64)), jnp.float32),
        "obs_anom": draw_obs_anom(jax.random.fold_in(keys[8], 71), 0),
        "innovation": draw_innovation(jax.random.fold_in(keys[8], 71), 0),
        "obs_precision": jnp.clip(jnp.exp(math.log(4.0) - 2.0794415 * jax.random.uniform(keys[4], (LAT_TILES, LON_TILES * OBS_DEV), jnp.float32) ** level_of(keys[4], (LAT_TILES, LON_TILES * OBS_DEV), ((0, 8), (1, 64)), -0.2, 0.2)), 0.5, 4.0).astype(jnp.bfloat16),
        "obs_blocks": with_ends(jax.random.randint(keys[5], (LAT_TILES, LON_TILES), 1, OBS_BLK + 1), jax.random.fold_in(keys[5], 1), 1, OBS_BLK).astype(jnp.int32),
        "localization": jnp.clip(jnp.exp(math.log(1.0) - 1.89712 * jax.random.uniform(keys[6], (LAT_TILES, LON_TILES * G, NEAR * OBS_DEV), jnp.float32) ** level_of(keys[6], (LAT_TILES, LON_TILES * G, NEAR * OBS_DEV), ((0, 8), (1, 64)), -0.2, 0.2)), 0.15, 1.0),
        "loc_pattern": with_ends((jax.random.randint(keys[7], (LAT_TILES, LON_TILES * G, NEAR * OBS_BLK), 0, 4) < 3).astype(jnp.int32), jax.random.fold_in(keys[7], 1), 0, 1),
    }


block_rows = 128
highest = lax.Precision.HIGHEST

def blend_table(groups, width):
    columns = np.arange(groups * width)
    offset = columns % width - (width - 1) / 2.0
    lower = np.where(offset < 0, columns // width, columns // width + 1)
    upper_share = np.where(offset < 0, (offset + width) / width, offset / width)
    slots = np.arange(groups + 2)[None, :]
    table = (1.0 - upper_share)[:, None] * (slots == lower[:, None]) + upper_share[:, None] * (slots == lower[:, None] + 1)
    return table.astype(np.float32)

def finish_weights(gram_matrix, projection, members):
    identity = jnp.eye(members, dtype=jnp.float32)
    system = gram_matrix + (members - 1.0) * identity
    bound = lax.optimization_barrier(jnp.max(lax.optimization_barrier(jnp.sum(jnp.abs(system), axis=2)), axis=1))
    current = system / bound[:, None, None]
    inverse_root = jnp.broadcast_to(identity, system.shape)
    for sweep in range(NSI):
        factor = 1.5 * identity - 0.5 * jnp.einsum('gij,gjk->gik', inverse_root, current, precision=highest)
        current = jnp.einsum('gij,gjk->gik', current, factor, precision=highest)
        inverse_root = jnp.einsum('gij,gjk->gik', factor, inverse_root, precision=highest)
    spread = inverse_root * jnp.sqrt((members - 1.0) / bound)[:, None, None]
    inner = jnp.einsum('gij,gj->gi', inverse_root, projection, precision=highest)
    centre = jnp.einsum('gij,gj->gi', inverse_root, inner, precision=highest) / bound[:, None]
    return spread + centre[:, :, None]

def group_weights(rows_y, rows_d, rows_r, local_weights, pattern, members):
    expanded = jnp.repeat(pattern, block_rows, axis=1).astype(jnp.float32)
    weights = local_weights * expanded * rows_r.astype(jnp.float32)[None, :]
    scaled = (rows_y.astype(jnp.float32)[None, :, :] * weights[:, :, None]).astype(jnp.bfloat16)
    gram_matrix = jnp.einsum('gnk,nl->gkl', scaled.astype(jnp.float32), rows_y.astype(jnp.float32))
    projection = jnp.einsum('gnk,n->gk', scaled.astype(jnp.float32), rows_d.astype(jnp.float32))
    return finish_weights(gram_matrix, projection, members)

def reference(anomalies, background_mean, obs_anom, innovation, obs_precision, obs_blocks, localization, loc_pattern):
    members = anomalies.shape[3]
    levels = anomalies.shape[2]
    tile_lat = anomalies.shape[0] // N_LAT
    tile_lon = anomalies.shape[1] // N_LON
    obs_rows = obs_anom.shape[1] // N_LON
    groups = localization.shape[1] // N_LON
    anom_tiles = obs_anom.reshape(N_LAT, N_LON, obs_rows, members)
    innov_tiles = innovation.reshape(N_LAT, N_LON, obs_rows)
    live = jnp.arange(obs_rows, dtype=jnp.int32)[None, None, :] < obs_blocks[:, :, None] * block_rows
    prec_tiles = obs_precision.reshape(N_LAT, N_LON, obs_rows) * live.astype(obs_precision.dtype)
    loc_tiles = localization.reshape(N_LAT, N_LON, groups, -1)
    pattern_tiles = loc_pattern.reshape(N_LAT, N_LON, groups, -1)

    def one_tile(tile_id):
        lat_tile = tile_id // N_LON
        lon_tile = tile_id % N_LON
        rows_y, rows_d, rows_r = ([], [], [])
        for lat_off in range(-LAT_REACH, LAT_REACH + 1):
            band = lat_tile + lat_off
            inside = (band >= 0) & (band < N_LAT)
            band = jnp.clip(band, 0, N_LAT - 1)
            for lon_off in range(-LON_REACH, LON_REACH + 1):
                column = (lon_tile + lon_off) % N_LON
                rows_y.append(anom_tiles[band, column])
                rows_d.append(innov_tiles[band, column])
                precision_here = prec_tiles[band, column]
                rows_r.append(jnp.where(inside, precision_here, jnp.zeros_like(precision_here)))
        return group_weights(jnp.concatenate(rows_y, 0), jnp.concatenate(rows_d, 0), jnp.concatenate(rows_r, 0), loc_tiles[lat_tile, lon_tile], pattern_tiles[lat_tile, lon_tile], members)
    tile_ids = jnp.arange(N_LAT * N_LON, dtype=jnp.int32)
    all_weights = lax.map(one_tile, tile_ids).reshape(N_LAT, N_LON, groups, members, members)
    table = jnp.asarray(blend_table(groups, tile_lon // groups), dtype=jnp.float32)

    def place(tile_id):
        lat_tile = tile_id // N_LON
        lon_tile = tile_id % N_LON
        left_edge = all_weights[lat_tile, (lon_tile - 1) % N_LON, groups - 1]
        right_edge = all_weights[lat_tile, (lon_tile + 1) % N_LON, 0]
        extended = jnp.concatenate([left_edge[None], all_weights[lat_tile, lon_tile], right_edge[None]], 0)
        column_weights = jnp.einsum('ce,eij->cij', table, extended, precision=highest).astype(jnp.bfloat16)
        zero_start = jnp.zeros((), jnp.int32)
        lat_start = (lat_tile * tile_lat).astype(jnp.int32)
        lon_start = (lon_tile * tile_lon).astype(jnp.int32)
        block = lax.dynamic_slice(anomalies, (lat_start, lon_start, zero_start, zero_start), (tile_lat, tile_lon, levels, members))
        mean_block = lax.dynamic_slice(background_mean, (lat_start, lon_start, zero_start), (tile_lat, tile_lon, levels))
        moved = jnp.einsum('acls,csk->aclk', block.astype(jnp.float32), column_weights.astype(jnp.float32))
        return (mean_block[..., None] + moved).astype(jnp.bfloat16)
    tiles = lax.map(place, tile_ids).reshape(N_LAT, N_LON, tile_lat, tile_lon, levels, members)
    return tiles.transpose(0, 2, 1, 3, 4, 5).reshape(N_LAT * tile_lat, N_LON * tile_lon, levels, members)
```

```python
import jax
import jax.numpy as jnp
import numpy as np
from jax import lax
from jax.experimental import pallas as pl
from jax.experimental.pallas import tpu as pltpu
from jax.sharding import PartitionSpec as P

LAT_REACH = 1
LON_REACH = 2
NSI = 5
BLOCK_ROWS = 128
SIDE = 2
TEAM = 4
EXTRA = 16
VMEM_LIMIT = 40 * 1024 * 1024

ACROSS = (((1,), (1,)), ((), ()))
PLAIN = (((1,), (0,)), ((), ()))
VMEM = pl.BlockSpec(memory_space=pltpu.VMEM)
SMEM = pl.BlockSpec(memory_space=pltpu.SMEM)


def params():
    return pltpu.CompilerParams(vmem_limit_bytes=VMEM_LIMIT)


def dot(a, b, dims=PLAIN):
    return lax.dot_general(a, b, dims, preferred_element_type=jnp.float32)


def split(x):
    high = x.astype(jnp.bfloat16)
    return high, (x - high.astype(jnp.float32)).astype(jnp.bfloat16)


def dot3(a, b):
    return dot(a[0], b[0]) + (dot(a[0], b[1]) + dot(a[1], b[0]))


def prepare_kernel(blocks_ref, anom_ref, innov_ref, prec_ref, out_ref):
    rows = anom_ref.shape[0]
    members = anom_ref.shape[1]
    out_ref[pl.ds(0, members), :] = anom_ref[...].T
    lane = lax.broadcasted_iota(jnp.int32, (1, rows), 1)
    live = (lane < blocks_ref[0, 0] * BLOCK_ROWS).astype(jnp.float32)
    innov = innov_ref[...].astype(jnp.float32)
    prec = prec_ref[...].astype(jnp.float32) * live
    row = lax.broadcasted_iota(jnp.int32, (EXTRA, rows), 0)
    tail = jnp.where(row == 0, innov, jnp.where(row == 1, prec, 0.0))
    out_ref[pl.ds(members, EXTRA), :] = tail.astype(jnp.bfloat16)


def gram_kernel(side_ref, weight_ref, *refs):
    out_ref = refs[-1]
    tiles = refs[:-1]
    members = tiles[0].shape[0] - EXTRA
    half = members // 2
    side = side_ref[0, 0]

    def share(dest, count):
        total = None
        for place in range(count):
            tile = tiles[place]
            weight = weight_ref[dest, pl.ds(place, 1), :] * tile[pl.ds(members + 1, 1), :].astype(jnp.float32)
            scaled = (tile[...].astype(jnp.float32) * weight).astype(jnp.bfloat16)
            part = dot(scaled, tile[pl.ds(0, members), :], ACROSS)
            total = part if total is None else total + part
        return total

    row = lax.broadcasted_iota(jnp.int32, (half, half), 0)
    col = lax.broadcasted_iota(jnp.int32, (half, half), 1)
    edge_row = lax.broadcasted_iota(jnp.int32, (EXTRA, members), 0)
    for step in range(TEAM):
        far = step < SIDE
        dest = (SIDE * (1 - side) if far else SIDE * side) + step % SIDE
        total = share(dest, len(tiles) if far else len(tiles) // 2)
        first = total[:half, :half]
        last = total[half:members, half:]
        out_ref[dest, pl.ds(0, half), pl.ds(0, half)] = jnp.where(row <= col, first, last).astype(jnp.bfloat16)
        out_ref[dest, pl.ds(0, half), pl.ds(half, half)] = total[:half, half:].astype(jnp.bfloat16)
        diagonal = jnp.sum(jnp.where(row == col, last, 0.0), axis=0, keepdims=True)
        diagonal = jnp.concatenate([diagonal, diagonal], axis=1)
        projection = total[members:members + 1, :]
        tail = jnp.where(edge_row == 0, projection, jnp.where(edge_row == 1, diagonal, 0.0))
        out_ref[dest, pl.ds(half, EXTRA), :] = tail.astype(jnp.bfloat16)


def transform_kernel(part_ref, own_ref, core_ref, cross_ref, own_out, core_out, cross_out):
    members = part_ref.shape[2]
    half = members // 2
    total = part_ref[0].astype(jnp.float32)
    for index in range(1, TEAM):
        total = total + part_ref[index].astype(jnp.float32)
    mixed = total[:half, :half]
    beside = total[:half, half:]
    projection = total[half:half + 1, :]
    row = lax.broadcasted_iota(jnp.int32, (half, half), 0)
    col = lax.broadcasted_iota(jnp.int32, (half, half), 1)
    mixed_t = mixed.T
    first = jnp.where(row <= col, mixed, mixed_t)
    last = jnp.where(row == col, total[half + 1:half + 2, :half], jnp.where(row > col, mixed, mixed_t))
    gram = jnp.concatenate(
        [jnp.concatenate([first, beside], axis=1), jnp.concatenate([beside.T, last], axis=1)], axis=0
    )
    row = lax.broadcasted_iota(jnp.int32, (members, members), 0)
    col = lax.broadcasted_iota(jnp.int32, (members, members), 1)
    identity = (row == col).astype(jnp.float32)
    system = gram + (members - 1.0) * identity
    bound = jnp.max(jnp.sum(jnp.abs(system), axis=0, keepdims=True), axis=1, keepdims=True)
    current = system / bound
    inverse_root = None
    for sweep in range(NSI):
        if sweep == 0:
            factor = 1.5 * identity - 0.5 * current
            inverse_root = factor
        else:
            factor = 1.5 * identity - 0.5 * dot3(root_parts, split(current))
        factor_parts = split(factor)
        if sweep < NSI - 1:
            current = dot3(split(current), factor_parts)
        if sweep > 0:
            inverse_root = dot3(factor_parts, root_parts)
        root_parts = split(inverse_root)
    inner = dot3(split(jnp.broadcast_to(projection, (8, members))), root_parts)
    centre = dot3(split(inner), root_parts) / bound
    transform = inverse_root * jnp.sqrt((members - 1.0) / bound) + centre.T[:, 0:1]
    transform = transform.astype(jnp.bfloat16)
    own_out[...] = dot(own_ref[...], transform)
    core_out[...] = dot(core_ref[...], transform).astype(jnp.bfloat16)
    cross_out[...] = dot(cross_ref[...], transform).astype(jnp.bfloat16)


def shifts(lat_count, lon_count, move):
    pairs = []
    for lat in range(lat_count):
        for lon in range(lon_count):
            target = move(lat, lon)
            if target is not None:
                pairs.append((lat * lon_count + lon, target[0] * lon_count + target[1]))
    return pairs


def local(
    anomalies,
    background_mean,
    obs_anom,
    innovation,
    obs_precision,
    obs_blocks,
    localization,
    loc_pattern,
):
    members = obs_anom.shape[2]
    obs_rows = obs_anom.shape[1]
    tile_lat, tile_lon, levels, _ = anomalies.shape
    half = members // 2
    lat_count = lax.axis_size("lat")
    lon_count = lax.axis_size("lon")
    reach = 2 * LON_REACH + 1
    near_lat = 2 * LAT_REACH + 1
    place = lax.axis_index("lon") % TEAM
    side = place // SIDE
    even = place % 2 == 0

    def send(value, move):
        return lax.ppermute(value, ("lat", "lon"), shifts(lat_count, lon_count, move))

    def moved_by(lat_step, team_step):
        def move(lat, lon):
            target = lat + lat_step
            if not 0 <= target < lat_count:
                return None
            step = 0 if not team_step else (TEAM if lon % TEAM >= SIDE else -TEAM)
            return target, (lon + step) % lon_count

        return move

    own = pl.pallas_call(
        prepare_kernel,
        out_shape=jax.ShapeDtypeStruct((members + EXTRA, obs_rows), jnp.bfloat16),
        in_specs=[SMEM, VMEM, VMEM, VMEM],
        out_specs=VMEM,
        compiler_params=params(),
        name="prepare",
    )(obs_blocks, obs_anom[0], innovation, obs_precision)

    tiles = []
    for team_step in (0, 1):
        for lat_off in range(-LAT_REACH, LAT_REACH + 1):
            if lat_off == 0 and not team_step:
                tiles.append(own)
            else:
                tiles.append(send(own, moved_by(-lat_off, team_step)))

    pattern = jnp.repeat(loc_pattern[0], BLOCK_ROWS, axis=1).astype(jnp.float32)
    weights = (localization[0] * pattern).reshape(near_lat, reach, obs_rows)
    weights = jnp.pad(weights, ((0, 0), (3, 3), (0, 0)))
    weights = lax.dynamic_slice_in_dim(weights, 3 - place, 2 * TEAM, axis=1)
    order = ((2, 6), (3, 7), (4, 0), (5, 1))
    weights = jnp.stack([jnp.concatenate([weights[:, a], weights[:, b]], 0) for a, b in order])
    teams = [[team * TEAM + i for i in range(TEAM)] for team in range(lon_count // TEAM)]
    weights = lax.all_to_all(weights, "lon", 0, 0, axis_index_groups=teams, tiled=True)

    shares = pl.pallas_call(
        gram_kernel,
        out_shape=jax.ShapeDtypeStruct((TEAM, half + EXTRA, members), jnp.bfloat16),
        in_specs=[SMEM] + [VMEM] * (1 + len(tiles)),
        out_specs=VMEM,
        compiler_params=params(),
        name="gram",
    )(side.reshape(1, 1).astype(jnp.int32), weights, *tiles)

    def core_move(lat, lon):
        return lat, lon ^ 1

    def cross_move(lat, lon):
        return lat, (lon + (1 if lon % 2 else -1)) % lon_count

    left = anomalies[:, : tile_lon // 2].reshape(-1, members)
    right = anomalies[:, tile_lon // 2 :].reshape(-1, members)
    core_cols = send(jnp.where(even, right, left), core_move)
    cross_cols = send(jnp.where(even, left, right), cross_move)

    shares = lax.all_to_all(shares, "lon", 0, 0, axis_index_groups=teams, tiled=True)

    moved, core_back, cross_back = pl.pallas_call(
        transform_kernel,
        out_shape=(
            jax.ShapeDtypeStruct((tile_lat * tile_lon * levels, members), jnp.float32),
            jax.ShapeDtypeStruct(core_cols.shape, jnp.bfloat16),
            jax.ShapeDtypeStruct(cross_cols.shape, jnp.bfloat16),
        ),
        in_specs=[VMEM] * 4,
        out_specs=(VMEM, VMEM, VMEM),
        compiler_params=params(),
        name="transform",
    )(shares, anomalies.reshape(-1, members), core_cols, cross_cols)

    cross_back = send(cross_back, cross_move)
    core_back = send(core_back, core_move)
    offset = np.abs(np.arange(tile_lon) - (tile_lon - 1) / 2.0) / tile_lon
    other_share = jnp.asarray(offset, jnp.float32)[None, :, None, None]
    moved = moved.reshape(anomalies.shape)
    part = (tile_lat, tile_lon // 2, levels, members)
    from_left = jnp.where(even, cross_back, core_back).reshape(part)
    from_right = jnp.where(even, core_back, cross_back).reshape(part)
    others = jnp.concatenate([from_left, from_right], 1).astype(jnp.float32)
    total = background_mean[..., None] + (1.0 - other_share) * moved + other_share * others
    return total.astype(jnp.bfloat16)


def solution(mesh):
    in_specs = (
        P("lat", "lon", None, None),
        P("lat", "lon", None),
        P("lat", "lon", None),
        P("lat", "lon"),
        P("lat", "lon"),
        P("lat", "lon"),
        P("lat", "lon", None),
        P("lat", "lon", None),
    )
    out_specs = P("lat", "lon", None, None)
    return jax.shard_map(local, mesh=mesh, in_specs=in_specs, out_specs=out_specs, check_vma=False)
```

```python
import jax
import jax.numpy as jnp
from jax import lax
from jax.experimental import pallas as pl
from jax.experimental.pallas import tpu as pltpu
from jax.sharding import PartitionSpec as P

LAT_REACH = 1
LON_REACH = 2
NEAR_LAT = 2 * LAT_REACH + 1
NEAR_LON = 2 * LON_REACH + 1
NSI = 5
BLOCK_ROWS = 128
SIDE = 2
TEAM = 4
EXTRA = 16
VMEM_LIMIT = 40 * 1024 * 1024

ACROSS = (((1,), (1,)), ((), ()))
PLAIN = (((1,), (0,)), ((), ()))
VMEM = pl.BlockSpec(memory_space=pltpu.VMEM)
SMEM = pl.BlockSpec(memory_space=pltpu.SMEM)
ANY = pl.BlockSpec(memory_space=pl.ANY)


def dot(a, b, dims=PLAIN):
    return lax.dot_general(a, b, dims, preferred_element_type=jnp.float32)


def split(x):
    high = x.astype(jnp.bfloat16)
    return high, (x - high.astype(jnp.float32)).astype(jnp.bfloat16)


def dot3(a, b):
    return dot(a[0], b[0]) + (dot(a[0], b[1]) + dot(a[1], b[0]))


def prepare_kernel(
    place_ref,
    blocks_ref,
    pattern_ref,
    anom_hbm,
    innov_hbm,
    prec_hbm,
    local_hbm,
    tile_ref,
    pack_ref,
    anom_ref,
    innov_ref,
    prec_ref,
    local_ref,
    weight_ref,
    sems,
):
    copies = []
    for index, (source, target) in enumerate(
        ((local_hbm, local_ref), (innov_hbm, innov_ref), (prec_hbm, prec_ref), (anom_hbm, anom_ref))
    ):
        copies.append(pltpu.make_async_copy(source, target, sems.at[index]))
        copies[-1].start()
    rows, members = anom_ref.shape
    place = place_ref[0, 0]
    blocks = rows // BLOCK_ROWS
    copies[0].wait()

    def weights(tiles):
        for kind, offset in enumerate(tiles):
            inside = (offset >= -LON_REACH) & (offset <= LON_REACH)
            offset = jnp.clip(offset, -LON_REACH, LON_REACH) + LON_REACH
            for lat in range(NEAR_LAT):
                near = lat * NEAR_LON + offset
                for block in range(blocks):
                    used = jnp.where(inside, pattern_ref[0, near * blocks + block], 0).astype(jnp.float32)
                    start = pl.multiple_of((near * blocks + block) * BLOCK_ROWS, BLOCK_ROWS)
                    weight_ref[pl.ds(kind * NEAR_LAT + lat, 1), pl.ds(block * BLOCK_ROWS, BLOCK_ROWS)] = (
                        local_ref[:, pl.ds(start, BLOCK_ROWS)] * used
                    )
        return weight_ref[...]

    weight_ref[...] = jnp.zeros_like(weight_ref)
    for reader in range(TEAM):
        beside = reader + (-TEAM if reader >= SIDE else TEAM)
        pack_ref[reader] = jnp.concatenate(split(weights((reader - place, beside - place))), axis=0)

    high, low = split(weights((0 * place, 1 - 2 * (place % 2))))
    copies[1].wait()
    copies[2].wait()
    lane = lax.broadcasted_iota(jnp.int32, (1, rows), 1)
    live = (lane < blocks_ref[0, 0] * BLOCK_ROWS).astype(jnp.float32)
    innov = innov_ref[...].astype(jnp.float32)
    prec = prec_ref[...].astype(jnp.float32) * live
    used = 2 * NEAR_LAT
    tail = [innov, prec, high.astype(jnp.float32)[:used], low.astype(jnp.float32)[:used]]
    tail.append(jnp.zeros((EXTRA - 2 - 2 * used, rows), jnp.float32))
    tile_ref[pl.ds(members, EXTRA), :] = jnp.concatenate(tail, axis=0).astype(jnp.bfloat16)
    copies[3].wait()
    tile_ref[pl.ds(0, members), :] = anom_ref[...].T


def pack_weights(pack_ref, dest):
    parts = pack_ref[dest].astype(jnp.float32)
    return parts[: EXTRA // 2] + parts[EXTRA // 2 :]


def outer_weights(place_ref, beside_ref, forward_ref):
    members = beside_ref.shape[0] - EXTRA
    place = place_ref[0, 0]
    used = 2 * NEAR_LAT
    direct = beside_ref[pl.ds(members, EXTRA), :].astype(jnp.float32)[2 : 2 + 2 * used]
    passed = forward_ref[...].astype(jnp.float32)[2 : 2 + 2 * used]
    outer = (place == 0) | (place == TEAM - 1)
    direct = direct[:NEAR_LAT] + direct[used : used + NEAR_LAT]
    passed = passed[NEAR_LAT:used] + passed[used + NEAR_LAT :]
    return jnp.where(outer, direct, passed)


def weighted(tile_ref, weight):
    members = tile_ref.shape[0] - EXTRA
    prec = tile_ref[pl.ds(members, EXTRA), :].astype(jnp.float32)[1:2]
    scaled = (tile_ref[...].astype(jnp.float32) * (weight * prec)).astype(jnp.bfloat16)
    return dot(scaled, tile_ref[pl.ds(0, members), :], ACROSS)


def early_kernel(place_ref, pack_ref, forward_ref, own_ref, below_ref, above_ref, beside_ref, out_ref):
    far = SIDE - place_ref[0, 0] // SIDE * SIDE
    for dest in range(TEAM):
        weight = pack_weights(pack_ref, dest)
        total = None
        for lat, tile_ref in enumerate((below_ref, own_ref, above_ref)):
            part = weighted(tile_ref, weight[lat : lat + 1])
            total = part if total is None else total + part
        out_ref[dest] = total
    row = NEAR_LAT + LAT_REACH
    for step in range(SIDE):
        weight = pack_weights(pack_ref, far + step)[row : row + 1]
        out_ref[far + step] += weighted(beside_ref, weight)
    weight = outer_weights(place_ref, beside_ref, forward_ref)
    out_ref[TEAM] = weighted(beside_ref, weight[LAT_REACH : LAT_REACH + 1])


def late_kernel(
    place_ref, pack_ref, forward_ref, beside_ref, below_ref, above_ref, share_ref, out_ref, side_ref, total_ref
):
    members = share_ref.shape[2]
    half = members // 2
    side = place_ref[0, 0] // SIDE
    far = SIDE - side * SIDE
    tiles = ((0, below_ref), (2 * LAT_REACH, above_ref))
    for step in range(SIDE):
        weight = pack_weights(pack_ref, far + step)
        total = share_ref[far + step]
        for lat, tile_ref in tiles:
            row = NEAR_LAT + lat
            total = total + weighted(tile_ref, weight[row : row + 1])
        total_ref[far + step] = total
        total_ref[SIDE - far + step] = share_ref[SIDE - far + step]
    weight = outer_weights(place_ref, beside_ref, forward_ref)
    total = share_ref[TEAM]
    for lat, tile_ref in tiles:
        total = total + weighted(tile_ref, weight[lat : lat + 1])
    total_ref[TEAM] = total

    row = lax.broadcasted_iota(jnp.int32, (half, half), 0)
    col = lax.broadcasted_iota(jnp.int32, (half, half), 1)

    def packed(total):
        first = total[:half, :half]
        last = total[half:members, half:]
        diagonal = jnp.sum(jnp.where(row == col, last, 0.0), axis=0, keepdims=True)
        body = jnp.concatenate([jnp.where(row <= col, first, last), total[:half, half:]], axis=1)
        tail = jnp.concatenate([total[members : members + 1], jnp.concatenate([diagonal, diagonal], axis=1)], axis=0)
        return body.astype(jnp.bfloat16), tail

    def padded(tails):
        rows = sum(tail.shape[0] for tail in tails)
        zeros = jnp.zeros((EXTRA - rows, members), jnp.float32)
        return jnp.concatenate([*tails, zeros], axis=0).astype(jnp.bfloat16)

    group = [packed(total_ref[dest]) for dest in range(TEAM)]
    outer = packed(total_ref[TEAM])

    def write(reader, parts):
        for slot, (body, _) in enumerate(parts):
            out_ref[reader, pl.ds(slot * half, half), :] = body
        out_ref[reader, pl.ds(members, EXTRA), :] = padded([tail for _, tail in parts])

    def write_side(part):
        side_ref[pl.ds(0, half), :] = part[0]
        side_ref[pl.ds(half, EXTRA), :] = padded([part[1]])

    nothing = tuple(jnp.zeros_like(part) for part in outer)
    write(1, (group[1], group[2]))
    write(2, (group[1], group[2]))

    @pl.when(side == 0)
    def _():
        write(0, (nothing, group[0]))
        write(3, (group[3], outer))
        write_side(group[3])

    @pl.when(side == 1)
    def _():
        write(0, (outer, group[0]))
        write(3, (group[3], nothing))
        write_side(group[0])


def transform_kernel(place_ref, part_ref, same_ref, other_ref, self_out, outer_out):
    members = part_ref.shape[2]
    half = members // 2
    place = place_ref[0, 0]
    total = part_ref[0].astype(jnp.float32)
    for index in range(1, TEAM):
        total = total + part_ref[index].astype(jnp.float32)
    side = same_ref[...].astype(jnp.float32) + other_ref[...].astype(jnp.float32)
    row = lax.broadcasted_iota(jnp.int32, (half, half), 0)
    col = lax.broadcasted_iota(jnp.int32, (half, half), 1)
    upper = row <= col
    diagonal = row == col
    full_row = lax.broadcasted_iota(jnp.int32, (members, members), 0)
    full_col = lax.broadcasted_iota(jnp.int32, (members, members), 1)
    identity = (full_row == full_col).astype(jnp.float32)

    systems, projections, bounds = [], [], []
    for slot in range(2):
        mine = (place < SIDE) if slot == 0 else (place >= SIDE)
        extra = jnp.where(mine, side, 0.0)
        body = total[slot * half : (slot + 1) * half] + extra[:half]
        tail = total[members + 2 * slot : members + 2 * slot + 2] + extra[half : half + 2]
        mixed = body[:, :half]
        beside = body[:, half:]
        mixed_t = mixed.T
        first = jnp.where(upper, mixed, mixed_t)
        last = jnp.where(diagonal, tail[1:2, :half], jnp.where(upper, mixed_t, mixed))
        gram = jnp.concatenate(
            [jnp.concatenate([first, beside], axis=1), jnp.concatenate([beside.T, last], axis=1)], axis=0
        )
        system = gram + (members - 1.0) * identity
        bound = jnp.max(jnp.sum(jnp.abs(system), axis=0, keepdims=True), axis=1, keepdims=True)
        systems.append(system / bound)
        projections.append(tail[0:1])
        bounds.append(bound)

    current = systems
    factor = [1.5 * identity - 0.5 * x for x in current]
    parts = [split(x) for x in factor]
    roots = parts
    for sweep in range(1, NSI):
        current = [dot3(split(x), f) for x, f in zip(current, parts)]
        factor = [1.5 * identity - 0.5 * dot3(r, split(x)) for r, x in zip(roots, current)]
        parts = [split(x) for x in factor]
        inverse_root = [dot3(f, r) for f, r in zip(parts, roots)]
        roots = [split(x) for x in inverse_root]
    transforms = []
    for root, parts, projection, bound in zip(inverse_root, roots, projections, bounds):
        inner = dot3(split(jnp.broadcast_to(projection, (8, members))), parts)
        centre = dot3(split(inner), parts) / bound
        transforms.append(root * jnp.sqrt((members - 1.0) / bound) + centre.T[:, 0:1])
    even = place % 2 == 0
    self_out[...] = jnp.where(even, transforms[1], transforms[0]).astype(jnp.bfloat16)
    outer_out[...] = jnp.where(even, transforms[0], transforms[1]).astype(jnp.bfloat16)


def other_shares(width):
    return [abs(column - (width - 1) / 2.0) / width for column in range(width)]


def moved_columns(state_ref, columns, transform_ref):
    tile_lat, _, levels, members = state_ref.shape
    rows = state_ref[:, columns].reshape(tile_lat * (columns.stop - columns.start) * levels, members)
    return dot(rows, transform_ref[...]).reshape(tile_lat, -1, levels, members)


def product_kernel(place_ref, self_ref, outer_ref, base_ref, state_ref, out_ref):
    width = state_ref.shape[1]
    half = width // 2
    shares = other_shares(width)
    moved = moved_columns(state_ref, slice(0, width), self_ref)

    def write(outer):
        beside = moved_columns(state_ref, outer, outer_ref)
        for column, other in enumerate(shares):
            value = base_ref[:, column] + (1.0 - other) * moved[:, column]
            if outer.start <= column < outer.stop:
                value = value + other * beside[:, column - outer.start]
            out_ref[:, column] = value

    even = place_ref[0, 0] % 2 == 0

    @pl.when(even)
    def _():
        write(slice(0, half))

    @pl.when(jnp.logical_not(even))
    def _():
        write(slice(half, width))


def blend_kernel(place_ref, inner_ref, part_ref, state_ref, out_ref):
    width = state_ref.shape[1]
    half = width // 2
    shares = other_shares(width)

    def write(inner):
        beside = moved_columns(state_ref, inner, inner_ref)
        for column, other in enumerate(shares):
            value = part_ref[:, column]
            if inner.start <= column < inner.stop:
                value = value + other * beside[:, column - inner.start]
            out_ref[:, column] = value.astype(jnp.bfloat16)

    even = place_ref[0, 0] % 2 == 0

    @pl.when(even)
    def _():
        write(slice(half, width))

    @pl.when(jnp.logical_not(even))
    def _():
        write(slice(0, half))


def shifts(lat_count, lon_count, move):
    pairs = []
    for lat in range(lat_count):
        for lon in range(lon_count):
            target = move(lat, lon)
            if target is not None and 0 <= target[0] < lat_count:
                pairs.append((lat * lon_count + lon, target[0] * lon_count + target[1] % lon_count))
    return pairs


def local(
    anomalies,
    background_mean,
    obs_anom,
    innovation,
    obs_precision,
    obs_blocks,
    localization,
    loc_pattern,
):
    members = obs_anom.shape[2]
    obs_rows = obs_anom.shape[1]
    half = members // 2
    lat_count = lax.axis_size("lat")
    lon_count = lax.axis_size("lon")
    teams = [[team * TEAM + i for i in range(TEAM)] for team in range(lon_count // TEAM)]
    place = (lax.axis_index("lon") % TEAM).astype(jnp.int32).reshape(1, 1)
    bf16, f32 = jnp.bfloat16, jnp.float32

    def call(kernel, outs, ins, *operands, scratch=(), limit=VMEM_LIMIT):
        return pl.pallas_call(
            kernel,
            out_shape=tuple(jax.ShapeDtypeStruct(*out) for out in outs),
            in_specs=ins,
            out_specs=(VMEM,) * len(outs),
            scratch_shapes=scratch,
            compiler_params=pltpu.CompilerParams(vmem_limit_bytes=limit),
            name=kernel.__name__.removesuffix("_kernel"),
        )(*operands)

    def send(value, move):
        return lax.ppermute(value, ("lat", "lon"), shifts(lat_count, lon_count, move))

    def exchange(value):
        return lax.all_to_all(value, "lon", 0, 0, axis_index_groups=teams, tiled=True)

    def up(lat, lon):
        return lat + 1, lon

    def down(lat, lon):
        return lat - 1, lon

    def other_core(lat, lon):
        return lat, lon ^ 1

    def along_x(lat, lon):
        return lat, lon + (TEAM if lon % TEAM >= SIDE else -TEAM)

    def back_same(lat, lon):
        step = {0: TEAM, TEAM - 1: -TEAM}.get(lon % TEAM)
        return None if step is None else (lat, lon + step)

    def back_other(lat, lon):
        step = {1: TEAM - 1, TEAM - 2: 1 - TEAM}.get(lon % TEAM)
        return None if step is None else (lat, lon + step)

    own, pack = call(
        prepare_kernel,
        [((members + EXTRA, obs_rows), bf16), ((TEAM, EXTRA, obs_rows), bf16)],
        [SMEM] * 3 + [ANY] * 4,
        place,
        obs_blocks,
        loc_pattern[0],
        obs_anom[0],
        innovation,
        obs_precision,
        localization[0],
        scratch=[
            pltpu.VMEM((obs_rows, members), bf16),
            pltpu.VMEM((1, obs_rows), bf16),
            pltpu.VMEM((1, obs_rows), bf16),
            pltpu.VMEM((1, localization.shape[2]), f32),
            pltpu.VMEM((EXTRA // 2, obs_rows), f32),
            pltpu.SemaphoreType.DMA((4,)),
        ],
        limit=56 * 1024 * 1024,
    )
    beside = send(own, along_x)
    below = send(own, up)
    above = send(own, down)
    pack = exchange(pack)
    beside_below = send(beside, up)
    beside_above = send(beside, down)
    forward = send(beside[members:], other_core)

    (shares,) = call(
        early_kernel,
        [((TEAM + 1, members + EXTRA, members), f32)],
        [SMEM] + [VMEM] * 6,
        place,
        pack,
        forward,
        own,
        below,
        above,
        beside,
    )
    shares, side = call(
        late_kernel,
        [((TEAM, members + EXTRA, members), bf16), ((half + EXTRA, members), bf16)],
        [SMEM] + [VMEM] * 6,
        place,
        pack,
        forward,
        beside,
        beside_below,
        beside_above,
        shares,
        scratch=[pltpu.VMEM((TEAM + 1, members + EXTRA, members), f32)],
    )
    shares = exchange(shares)
    same = send(side, back_same)
    other = send(side, back_other)

    transform, outer = call(
        transform_kernel,
        [((members, members), bf16)] * 2,
        [SMEM] + [VMEM] * 3,
        place,
        shares,
        same,
        other,
    )
    inner = send(transform, other_core)
    base = jnp.broadcast_to(background_mean[..., None], anomalies.shape)
    (part,) = call(
        product_kernel, [(anomalies.shape, f32)], [SMEM] + [VMEM] * 4, place, transform, outer, base, anomalies
    )
    (analysis,) = call(blend_kernel, [(anomalies.shape, bf16)], [SMEM] + [VMEM] * 3, place, inner, part, anomalies)
    return analysis


def solution(mesh):
    in_specs = (
        P("lat", "lon", None, None),
        P("lat", "lon", None),
        P("lat", "lon", None),
        P("lat", "lon"),
        P("lat", "lon"),
        P("lat", "lon"),
        P("lat", "lon", None),
        P("lat", "lon", None),
    )
    out_specs = P("lat", "lon", None, None)
    return jax.shard_map(local, mesh=mesh, in_specs=in_specs, out_specs=out_specs, check_vma=False)
```

```python
import jax
import jax.numpy as jnp
from jax import lax
from jax.experimental import pallas as pl
from jax.experimental.pallas import tpu as pltpu
from jax.sharding import PartitionSpec as P

LAT_REACH = 1
LON_REACH = 2
NEAR_LAT = 2 * LAT_REACH + 1
NEAR_LON = 2 * LON_REACH + 1
NSI = 5
BLOCK_ROWS = 128
SIDE = 2
TEAM = 4
EXTRA = 16
VMEM_LIMIT = 40 * 1024 * 1024

ACROSS = (((1,), (1,)), ((), ()))
PLAIN = (((1,), (0,)), ((), ()))
VMEM = pl.BlockSpec(memory_space=pltpu.VMEM)
SMEM = pl.BlockSpec(memory_space=pltpu.SMEM)
ANY = pl.BlockSpec(memory_space=pl.ANY)


def dot(a, b, dims=PLAIN):
    return lax.dot_general(a, b, dims, preferred_element_type=jnp.float32)


def split(x):
    high = x.astype(jnp.bfloat16)
    return high, (x - high.astype(jnp.float32)).astype(jnp.bfloat16)


def dot3(a, b):
    return dot(a[0], b[0]) + (dot(a[0], b[1]) + dot(a[1], b[0]))


def prepare_kernel(
    place_ref,
    blocks_ref,
    pattern_ref,
    anom_hbm,
    innov_hbm,
    prec_hbm,
    local_hbm,
    tile_ref,
    pack_ref,
    anom_ref,
    innov_ref,
    prec_ref,
    local_ref,
    weight_ref,
    sems,
):
    copies = []
    for index, (source, target) in enumerate(
        ((local_hbm, local_ref), (innov_hbm, innov_ref), (prec_hbm, prec_ref), (anom_hbm, anom_ref))
    ):
        copies.append(pltpu.make_async_copy(source, target, sems.at[index]))
        copies[-1].start()
    rows, members = anom_ref.shape
    place = place_ref[0, 0]
    blocks = rows // BLOCK_ROWS
    copies[0].wait()

    def weights(tiles):
        for kind, offset in enumerate(tiles):
            inside = (offset >= -LON_REACH) & (offset <= LON_REACH)
            offset = jnp.clip(offset, -LON_REACH, LON_REACH) + LON_REACH
            for lat in range(NEAR_LAT):
                near = lat * NEAR_LON + offset
                for block in range(blocks):
                    used = jnp.where(inside, pattern_ref[0, near * blocks + block], 0).astype(jnp.float32)
                    start = pl.multiple_of((near * blocks + block) * BLOCK_ROWS, BLOCK_ROWS)
                    weight_ref[pl.ds(kind * NEAR_LAT + lat, 1), pl.ds(block * BLOCK_ROWS, BLOCK_ROWS)] = (
                        local_ref[:, pl.ds(start, BLOCK_ROWS)] * used
                    )
        return weight_ref[...]

    weight_ref[...] = jnp.zeros_like(weight_ref)
    for reader in range(TEAM):
        beside = reader + (-TEAM if reader >= SIDE else TEAM)
        pack_ref[reader] = jnp.concatenate(split(weights((reader - place, beside - place))), axis=0)

    high, low = split(weights((0 * place, 1 - 2 * (place % 2))))
    copies[1].wait()
    copies[2].wait()
    lane = lax.broadcasted_iota(jnp.int32, (1, rows), 1)
    live = (lane < blocks_ref[0, 0] * BLOCK_ROWS).astype(jnp.float32)
    innov = innov_ref[...].astype(jnp.float32)
    prec = prec_ref[...].astype(jnp.float32) * live
    used = 2 * NEAR_LAT
    tail = [innov, prec, high.astype(jnp.float32)[:used], low.astype(jnp.float32)[:used]]
    tail.append(jnp.zeros((EXTRA - 2 - 2 * used, rows), jnp.float32))
    tile_ref[pl.ds(members, EXTRA), :] = jnp.concatenate(tail, axis=0).astype(jnp.bfloat16)
    copies[3].wait()
    tile_ref[pl.ds(0, members), :] = anom_ref[...].T


def joined(pack):
    parts = pack.astype(jnp.float32)
    return parts[: EXTRA // 2] + parts[EXTRA // 2 :]


def team_weights(place_ref, pack_ref, cross_ref, core_ref, index):
    return joined(
        (
            lambda: pack_ref[place_ref[0, 0]],
            lambda: core_ref[0],
            lambda: cross_ref[0],
            lambda: core_ref[1],
        )[index]()
    )


def outer_weights(place_ref, beside_ref, core_ref):
    members = beside_ref.shape[0] - EXTRA
    place = place_ref[0, 0]
    used = 2 * NEAR_LAT
    direct = beside_ref[pl.ds(members, EXTRA), :].astype(jnp.float32)[2 : 2 + 2 * used]
    passed = core_ref[2].astype(jnp.float32)[2 : 2 + 2 * used]
    outer = (place == 0) | (place == TEAM - 1)
    direct = direct[:NEAR_LAT] + direct[used : used + NEAR_LAT]
    passed = passed[NEAR_LAT:used] + passed[used + NEAR_LAT :]
    return jnp.where(outer, direct, passed)


def weighted(tile_ref, weight):
    members = tile_ref.shape[0] - EXTRA
    prec = tile_ref[pl.ds(members, EXTRA), :].astype(jnp.float32)[1:2]
    scaled = (tile_ref[...].astype(jnp.float32) * (weight * prec)).astype(jnp.bfloat16)
    return dot(scaled, tile_ref[pl.ds(0, members), :], ACROSS)


def early_kernel(
    place_ref, pack_ref, cross_ref, core_ref, own_ref, below_ref, above_ref, beside_ref, out_ref
):
    for index in range(TEAM):
        weight = team_weights(place_ref, pack_ref, cross_ref, core_ref, index)
        total = None
        for lat, tile_ref in enumerate((below_ref, own_ref, above_ref)):
            part = weighted(tile_ref, weight[lat : lat + 1])
            total = part if total is None else total + part
        if index >= SIDE:
            row = NEAR_LAT + LAT_REACH
            total = total + weighted(beside_ref, weight[row : row + 1])
        out_ref[index] = total
    weight = outer_weights(place_ref, beside_ref, core_ref)
    out_ref[TEAM] = weighted(beside_ref, weight[LAT_REACH : LAT_REACH + 1])


def packed(total):
    members = total.shape[1]
    half = members // 2
    row = lax.broadcasted_iota(jnp.int32, (half, half), 0)
    col = lax.broadcasted_iota(jnp.int32, (half, half), 1)
    first = total[:half, :half]
    last = total[half:members, half:]
    diagonal = jnp.sum(jnp.where(row == col, last, 0.0), axis=0, keepdims=True)
    body = jnp.concatenate([jnp.where(row <= col, first, last), total[:half, half:]], axis=1)
    return body, jnp.concatenate(
        [total[members : members + 1], jnp.concatenate([diagonal, diagonal], axis=1)], axis=0
    )


def put(out_ref, parts):
    half, members = next(part[0].shape for part in parts if part is not None)
    tails = []
    for slot, part in enumerate(parts):
        body, tail = part or (jnp.zeros((half, members), jnp.float32), jnp.zeros((2, members), jnp.float32))
        out_ref[pl.ds(slot * half, half), :] = body.astype(out_ref.dtype)
        tails.append(tail)
    tails.append(jnp.zeros((EXTRA - 2 * len(parts), members), jnp.float32))
    out_ref[pl.ds(len(parts) * half, EXTRA), :] = jnp.concatenate(tails, axis=0).astype(out_ref.dtype)


def late_kernel(
    place_ref,
    cross_ref,
    core_ref,
    beside_ref,
    below_ref,
    above_ref,
    share_ref,
    give_ref,
    keep_ref,
    body_ref,
    tail_ref,
):
    tiles = ((0, below_ref), (2 * LAT_REACH, above_ref))
    for index in range(TEAM + 1):
        total = share_ref[index]
        if index >= SIDE:
            if index < TEAM:
                weight = joined(cross_ref[0] if index == SIDE else core_ref[1])[NEAR_LAT:]
            else:
                weight = outer_weights(place_ref, beside_ref, core_ref)
            for lat, tile_ref in tiles:
                total = total + weighted(tile_ref, weight[lat : lat + 1])
        body, tail = packed(total)
        body_ref[index] = body
        tail_ref[index, pl.ds(0, 2), :] = tail

    def write(place):
        def part(index):
            return body_ref[index], tail_ref[index, pl.ds(0, 2), :]

        middle = [part(1 ^ place), part(2 ^ place)]
        if place in (0, TEAM - 1):
            put(give_ref, (*middle, part(3), part(TEAM)))
            put(keep_ref, (*middle, part(0), None))
        else:
            put(give_ref, (*middle, part(1), None))
            put(keep_ref, (*middle, part(2), part(TEAM)))

    for place in range(TEAM):
        pl.when(place_ref[0, 0] == place)(lambda place=place: write(place))


def gather_kernel(place_ref, keep_ref, give_ref, cross_out, keep_out, side_out):
    half = (keep_ref.shape[0] - EXTRA) // 4
    total = keep_ref[...] + give_ref[...].astype(jnp.float32)
    tails = total[4 * half :]
    parts = [(total[slot * half : (slot + 1) * half], tails[2 * slot : 2 * slot + 2]) for slot in range(4)]

    def write(place):
        middle, ends = parts[:2], parts[2:]
        if place in (0, TEAM - 1):
            put(cross_out, middle)
            put(keep_out, (None, ends[0]) if place == 0 else (ends[0], None))
        else:
            put(cross_out, ends if place == 1 else ends[::-1])
            put(keep_out, middle)
        put(side_out, ends[:1])

    for place in range(TEAM):
        pl.when(place_ref[0, 0] == place)(lambda place=place: write(place))


def transform_kernel(place_ref, keep_ref, cross_ref, side_ref, self_out, outer_out):
    members = keep_ref.shape[1]
    half = members // 2
    place = place_ref[0, 0]
    total = keep_ref[...] + cross_ref[...].astype(jnp.float32)
    side = side_ref[...].astype(jnp.float32)
    row = lax.broadcasted_iota(jnp.int32, (half, half), 0)
    col = lax.broadcasted_iota(jnp.int32, (half, half), 1)
    upper = row <= col
    diagonal = row == col
    full_row = lax.broadcasted_iota(jnp.int32, (members, members), 0)
    full_col = lax.broadcasted_iota(jnp.int32, (members, members), 1)
    identity = (full_row == full_col).astype(jnp.float32)

    systems, projections, bounds = [], [], []
    for slot in range(2):
        mine = (place < SIDE) if slot == 0 else (place >= SIDE)
        extra = jnp.where(mine, side, 0.0)
        body = total[slot * half : (slot + 1) * half] + extra[:half]
        tail = total[members + 2 * slot : members + 2 * slot + 2] + extra[half : half + 2]
        mixed = body[:, :half]
        beside = body[:, half:]
        mixed_t = mixed.T
        first = jnp.where(upper, mixed, mixed_t)
        last = jnp.where(diagonal, tail[1:2, :half], jnp.where(upper, mixed_t, mixed))
        gram = jnp.concatenate(
            [jnp.concatenate([first, beside], axis=1), jnp.concatenate([beside.T, last], axis=1)], axis=0
        )
        system = gram + (members - 1.0) * identity
        bound = jnp.max(jnp.sum(jnp.abs(system), axis=0, keepdims=True), axis=1, keepdims=True)
        systems.append(system / bound)
        projections.append(tail[0:1])
        bounds.append(bound)

    current = systems
    factor = [1.5 * identity - 0.5 * x for x in current]
    parts = [split(x) for x in factor]
    roots = parts
    for sweep in range(1, NSI):
        current = [dot3(split(x), f) for x, f in zip(current, parts)]
        factor = [1.5 * identity - 0.5 * dot3(r, split(x)) for r, x in zip(roots, current)]
        parts = [split(x) for x in factor]
        inverse_root = [dot3(f, r) for f, r in zip(parts, roots)]
        roots = [split(x) for x in inverse_root]
    transforms = []
    for root, parts, projection, bound in zip(inverse_root, roots, projections, bounds):
        inner = dot3(split(jnp.broadcast_to(projection, (8, members))), parts)
        centre = dot3(split(inner), parts) / bound
        transforms.append(root * jnp.sqrt((members - 1.0) / bound) + centre.T[:, 0:1])
    even = place % 2 == 0
    self_out[...] = jnp.where(even, transforms[1], transforms[0]).astype(jnp.bfloat16)
    outer_out[...] = jnp.where(even, transforms[0], transforms[1]).astype(jnp.bfloat16)


def other_shares(width):
    return [abs(column - (width - 1) / 2.0) / width for column in range(width)]


def moved_columns(state_ref, columns, transform_ref):
    tile_lat, _, levels, members = state_ref.shape
    rows = state_ref[:, columns].reshape(tile_lat * (columns.stop - columns.start) * levels, members)
    return dot(rows, transform_ref[...]).reshape(tile_lat, -1, levels, members)


def product_kernel(place_ref, self_ref, outer_ref, base_ref, state_ref, out_ref):
    width = state_ref.shape[1]
    half = width // 2
    shares = other_shares(width)
    moved = moved_columns(state_ref, slice(0, width), self_ref)

    def write(outer):
        beside = moved_columns(state_ref, outer, outer_ref)
        for column, other in enumerate(shares):
            value = base_ref[:, column] + (1.0 - other) * moved[:, column]
            if outer.start <= column < outer.stop:
                value = value + other * beside[:, column - outer.start]
            out_ref[:, column] = value

    even = place_ref[0, 0] % 2 == 0

    @pl.when(even)
    def _():
        write(slice(0, half))

    @pl.when(jnp.logical_not(even))
    def _():
        write(slice(half, width))


def blend_kernel(place_ref, inner_ref, part_ref, state_ref, out_ref):
    width = state_ref.shape[1]
    half = width // 2
    shares = other_shares(width)

    def write(inner):
        beside = moved_columns(state_ref, inner, inner_ref)
        for column, other in enumerate(shares):
            value = part_ref[:, column]
            if inner.start <= column < inner.stop:
                value = value + other * beside[:, column - inner.start]
            out_ref[:, column] = value.astype(jnp.bfloat16)

    even = place_ref[0, 0] % 2 == 0

    @pl.when(even)
    def _():
        write(slice(half, width))

    @pl.when(jnp.logical_not(even))
    def _():
        write(slice(0, half))


def shifts(lat_count, lon_count, move):
    pairs = []
    for lat in range(lat_count):
        for lon in range(lon_count):
            target = move(lat, lon)
            if target is not None and 0 <= target[0] < lat_count:
                pairs.append((lat * lon_count + lon, target[0] * lon_count + target[1] % lon_count))
    return pairs


def local(
    anomalies,
    background_mean,
    obs_anom,
    innovation,
    obs_precision,
    obs_blocks,
    localization,
    loc_pattern,
):
    members = obs_anom.shape[2]
    obs_rows = obs_anom.shape[1]
    half = members // 2
    lat_count = lax.axis_size("lat")
    lon_count = lax.axis_size("lon")
    place = (lax.axis_index("lon") % TEAM).astype(jnp.int32).reshape(1, 1)
    bf16, f32 = jnp.bfloat16, jnp.float32

    def call(kernel, outs, ins, *operands, scratch=(), limit=VMEM_LIMIT):
        return pl.pallas_call(
            kernel,
            out_shape=tuple(jax.ShapeDtypeStruct(*out) for out in outs),
            in_specs=ins,
            out_specs=(VMEM,) * len(outs),
            scratch_shapes=scratch,
            compiler_params=pltpu.CompilerParams(vmem_limit_bytes=limit),
            name=kernel.__name__.removesuffix("_kernel"),
        )(*operands)

    def send(value, move):
        return lax.ppermute(value, ("lat", "lon"), shifts(lat_count, lon_count, move))

    def up(lat, lon):
        return lat + 1, lon

    def down(lat, lon):
        return lat - 1, lon

    def other_core(lat, lon):
        return lat, lon ^ 1

    def along_x(lat, lon):
        return lat, lon + (TEAM if lon % TEAM >= SIDE else -TEAM)

    def across_z(lat, lon):
        return lat, lon ^ 2

    def side_move(lat, lon):
        step = {1: TEAM - 1, TEAM - 2: 1 - TEAM}.get(lon % TEAM)
        return None if step is None else (lat, lon + step)

    own, pack = call(
        prepare_kernel,
        [((members + EXTRA, obs_rows), bf16), ((TEAM, EXTRA, obs_rows), bf16)],
        [SMEM] * 3 + [ANY] * 4,
        place,
        obs_blocks,
        loc_pattern[0],
        obs_anom[0],
        innovation,
        obs_precision,
        localization[0],
        scratch=[
            pltpu.VMEM((obs_rows, members), bf16),
            pltpu.VMEM((1, obs_rows), bf16),
            pltpu.VMEM((1, obs_rows), bf16),
            pltpu.VMEM((1, localization.shape[2]), f32),
            pltpu.VMEM((EXTRA // 2, obs_rows), f32),
            pltpu.SemaphoreType.DMA((4,)),
        ],
        limit=56 * 1024 * 1024,
    )
    index = place[0, 0]
    far = jnp.where(index % 2 == 0, jnp.stack([pack[2], pack[3]]), jnp.stack([pack[3], pack[2]]))
    near = jnp.where(index % 2 == 0, jnp.stack([pack[0], pack[1]]), jnp.stack([pack[1], pack[0]]))
    far, near = jnp.where(index < SIDE, far, near), jnp.where(index < SIDE, near, far)
    cross = send(far, across_z)
    beside = send(own, along_x)
    below = send(own, up)
    above = send(own, down)
    beside_below = send(beside, up)
    beside_above = send(beside, down)
    core = send(jnp.stack([near[1], cross[1], beside[members:]]), other_core)

    (shares,) = call(
        early_kernel,
        [((TEAM + 1, members + EXTRA, members), f32)],
        [SMEM] + [VMEM] * 7,
        place,
        pack,
        cross,
        core,
        own,
        below,
        above,
        beside,
    )
    give, keep = call(
        late_kernel,
        [((4 * half + EXTRA, members), bf16), ((4 * half + EXTRA, members), f32)],
        [SMEM] + [VMEM] * 6,
        place,
        cross,
        core,
        beside,
        beside_below,
        beside_above,
        shares,
        scratch=[pltpu.VMEM((TEAM + 1, half, members), f32), pltpu.VMEM((TEAM + 1, 8, members), f32)],
    )
    give = send(give, other_core)
    shares, keep, side = call(
        gather_kernel,
        [((members + EXTRA, members), bf16), ((members + EXTRA, members), f32), ((half + EXTRA, members), bf16)],
        [SMEM] + [VMEM] * 2,
        place,
        keep,
        give,
    )
    shares = send(shares, across_z)
    side = send(side, side_move)

    transform, outer = call(
        transform_kernel,
        [((members, members), bf16)] * 2,
        [SMEM] + [VMEM] * 3,
        place,
        keep,
        shares,
        side,
    )
    inner = send(transform, other_core)
    base = jnp.broadcast_to(background_mean[..., None], anomalies.shape)
    (part,) = call(
        product_kernel, [(anomalies.shape, f32)], [SMEM] + [VMEM] * 4, place, transform, outer, base, anomalies
    )
    (analysis,) = call(blend_kernel, [(anomalies.shape, bf16)], [SMEM] + [VMEM] * 3, place, inner, part, anomalies)
    return analysis


def solution(mesh):
    in_specs = (
        P("lat", "lon", None, None),
        P("lat", "lon", None),
        P("lat", "lon", None),
        P("lat", "lon"),
        P("lat", "lon"),
        P("lat", "lon"),
        P("lat", "lon", None),
        P("lat", "lon", None),
    )
    out_specs = P("lat", "lon", None, None)
    return jax.shard_map(local, mesh=mesh, in_specs=in_specs, out_specs=out_specs, check_vma=False)
```

```python
import jax
import jax.numpy as jnp
from jax import lax
from jax.experimental import pallas as pl
from jax.experimental.pallas import tpu as pltpu
from jax.sharding import PartitionSpec as P

LAT_REACH = 1
LON_REACH = 2
NEAR_LAT = 2 * LAT_REACH + 1
NEAR_LON = 2 * LON_REACH + 1
NSI = 5
BLOCK_ROWS = 128
SIDE = 2
TEAM = 4
EXTRA = 16
RELAY_ROWS = 208
VMEM_LIMIT = 32 * 1024 * 1024

ACROSS = (((1,), (1,)), ((), ()))
PLAIN = (((1,), (0,)), ((), ()))
VMEM = pl.BlockSpec(memory_space=pltpu.VMEM)
SMEM = pl.BlockSpec(memory_space=pltpu.SMEM)
ANY = pl.BlockSpec(memory_space=pl.ANY)


def dot(a, b, dims=PLAIN):
    return lax.dot_general(a, b, dims, preferred_element_type=jnp.float32)


def split(x):
    high = x.astype(jnp.bfloat16)
    return high, (x - high.astype(jnp.float32)).astype(jnp.bfloat16)


def dot3(a, b):
    return dot(a[0], b[0]) + (dot(a[0], b[1]) + dot(a[1], b[0]))


def prepare_kernel(
    place_ref,
    blocks_ref,
    pattern_ref,
    anom_hbm,
    innov_hbm,
    prec_hbm,
    local_hbm,
    tile_ref,
    near_ref,
    far_ref,
    anom_ref,
    innov_ref,
    prec_ref,
    local_ref,
    weight_ref,
    sems,
):
    copies = []
    for index, (source, target) in enumerate(
        ((local_hbm, local_ref), (innov_hbm, innov_ref), (prec_hbm, prec_ref), (anom_hbm, anom_ref))
    ):
        copies.append(pltpu.make_async_copy(source, target, sems.at[index]))
        copies[-1].start()
    rows, members = anom_ref.shape
    place = place_ref[0, 0]
    blocks = rows // BLOCK_ROWS
    copies[0].wait()

    def weights(tiles):
        for kind, offset in enumerate(tiles):
            inside = (offset >= -LON_REACH) & (offset <= LON_REACH)
            offset = jnp.clip(offset, -LON_REACH, LON_REACH) + LON_REACH
            for lat in range(NEAR_LAT):
                near = lat * NEAR_LON + offset
                for block in range(blocks):
                    used = jnp.where(inside, pattern_ref[0, near * blocks + block], 0).astype(jnp.float32)
                    start = pl.multiple_of((near * blocks + block) * BLOCK_ROWS, BLOCK_ROWS)
                    weight_ref[pl.ds(kind * NEAR_LAT + lat, 1), pl.ds(block * BLOCK_ROWS, BLOCK_ROWS)] = (
                        local_ref[:, pl.ds(start, BLOCK_ROWS)] * used
                    )
        return weight_ref[...]

    weight_ref[...] = jnp.zeros_like(weight_ref)
    for index in range(TEAM):
        reader = place ^ index
        beside = reader + jnp.where(reader >= SIDE, -TEAM, TEAM)
        pack_ref = near_ref if index < SIDE else far_ref
        pack_ref[index % SIDE] = jnp.concatenate(split(weights((reader - place, beside - place))), axis=0)

    high, low = split(weights((0 * place, 1 - 2 * (place % 2))))
    copies[1].wait()
    copies[2].wait()
    lane = lax.broadcasted_iota(jnp.int32, (1, rows), 1)
    live = (lane < blocks_ref[0, 0] * BLOCK_ROWS).astype(jnp.float32)
    innov = innov_ref[...].astype(jnp.float32)
    prec = prec_ref[...].astype(jnp.float32) * live
    used = 2 * NEAR_LAT
    tail = [innov, prec, high.astype(jnp.float32)[:used], low.astype(jnp.float32)[:used]]
    tail.append(jnp.zeros((EXTRA - 2 - 2 * used, rows), jnp.float32))
    tile_ref[pl.ds(members, EXTRA), :] = jnp.concatenate(tail, axis=0).astype(jnp.bfloat16)
    copies[3].wait()
    tile_ref[pl.ds(0, members), :] = anom_ref[...].T


def joined(pack):
    parts = pack.astype(jnp.float32)
    return parts[: EXTRA // 2] + parts[EXTRA // 2 :]


def relay_kernel(near_ref, cross_ref, beside_ref, out_ref):
    depth = beside_ref.shape[0]
    out_ref[pl.ds(0, EXTRA), :] = near_ref[1]
    out_ref[pl.ds(EXTRA, EXTRA), :] = cross_ref[1]
    out_ref[pl.ds(2 * EXTRA, RELAY_ROWS), :] = beside_ref[pl.ds(depth - RELAY_ROWS, RELAY_ROWS), :]


def outer_weights(place_ref, beside_ref, core_ref):
    members = beside_ref.shape[0] - EXTRA
    place = place_ref[0, 0]
    used = 2 * NEAR_LAT
    direct = beside_ref[pl.ds(members, EXTRA), :].astype(jnp.float32)[2 : 2 + 2 * used]
    passed = core_ref[pl.ds(core_ref.shape[0] - EXTRA, EXTRA), :].astype(jnp.float32)[2 : 2 + 2 * used]
    outer = (place == 0) | (place == TEAM - 1)
    direct = direct[:NEAR_LAT] + direct[used : used + NEAR_LAT]
    passed = passed[NEAR_LAT:used] + passed[used + NEAR_LAT :]
    return jnp.where(outer, direct, passed)


def weighted(tile_ref, weight):
    members = tile_ref.shape[0] - EXTRA
    prec = tile_ref[pl.ds(members, EXTRA), :].astype(jnp.float32)[1:2]
    scaled = (tile_ref[...].astype(jnp.float32) * (weight * prec)).astype(jnp.bfloat16)
    return dot(scaled, tile_ref[pl.ds(0, members), :], ACROSS)


def early_kernel(
    place_ref, near_ref, cross_ref, core_ref, own_ref, below_ref, above_ref, beside_ref, out_ref
):
    for index, pack in enumerate((near_ref[0], core_ref[pl.ds(0, EXTRA), :], cross_ref[0], core_ref[pl.ds(EXTRA, EXTRA), :])):
        weight = joined(pack)
        total = None
        for lat, tile_ref in enumerate((below_ref, own_ref, above_ref)):
            part = weighted(tile_ref, weight[lat : lat + 1])
            total = part if total is None else total + part
        if index >= SIDE:
            row = NEAR_LAT + LAT_REACH
            total = total + weighted(beside_ref, weight[row : row + 1])
        out_ref[index] = total
    weight = outer_weights(place_ref, beside_ref, core_ref)
    out_ref[TEAM] = weighted(beside_ref, weight[LAT_REACH : LAT_REACH + 1])


def packed(total):
    members = total.shape[1]
    half = members // 2
    row = lax.broadcasted_iota(jnp.int32, (half, half), 0)
    col = lax.broadcasted_iota(jnp.int32, (half, half), 1)
    first = total[:half, :half]
    last = total[half:members, half:]
    diagonal = jnp.sum(jnp.where(row == col, last, 0.0), axis=0, keepdims=True)
    body = jnp.concatenate([jnp.where(row <= col, first, last), total[:half, half:]], axis=1)
    return body, jnp.concatenate(
        [total[members : members + 1], jnp.concatenate([diagonal, diagonal], axis=1)], axis=0
    )


def put(out_ref, parts):
    half, members = next(part[0].shape for part in parts if part is not None)
    tails = []
    for slot, part in enumerate(parts):
        body, tail = part or (jnp.zeros((half, members), jnp.float32), jnp.zeros((2, members), jnp.float32))
        out_ref[pl.ds(slot * half, half), :] = body.astype(out_ref.dtype)
        tails.append(tail)
    tails.append(jnp.zeros((EXTRA - 2 * len(parts), members), jnp.float32))
    out_ref[pl.ds(len(parts) * half, EXTRA), :] = jnp.concatenate(tails, axis=0).astype(out_ref.dtype)


def late_kernel(
    place_ref,
    cross_ref,
    core_ref,
    beside_ref,
    below_ref,
    above_ref,
    share_ref,
    give_ref,
    keep_ref,
    body_ref,
    tail_ref,
):
    tiles = ((0, below_ref), (2 * LAT_REACH, above_ref))
    for index in range(TEAM + 1):
        total = share_ref[index]
        if index >= SIDE:
            if index < TEAM:
                weight = joined(cross_ref[0] if index == SIDE else core_ref[pl.ds(EXTRA, EXTRA), :])[NEAR_LAT:]
            else:
                weight = outer_weights(place_ref, beside_ref, core_ref)
            for lat, tile_ref in tiles:
                total = total + weighted(tile_ref, weight[lat : lat + 1])
        body, tail = packed(total)
        body_ref[index] = body
        tail_ref[index, pl.ds(0, 2), :] = tail

    def write(place):
        def part(index):
            return body_ref[index], tail_ref[index, pl.ds(0, 2), :]

        middle = [part(1 ^ place), part(2 ^ place)]
        if place in (0, TEAM - 1):
            put(give_ref, (*middle, part(3), part(TEAM)))
            put(keep_ref, (*middle, part(0), None))
        else:
            put(give_ref, (*middle, part(1), None))
            put(keep_ref, (*middle, part(2), part(TEAM)))

    for place in range(TEAM):
        pl.when(place_ref[0, 0] == place)(lambda place=place: write(place))


def gather_kernel(place_ref, keep_ref, give_ref, cross_out, keep_out, side_out):
    half = (keep_ref.shape[0] - EXTRA) // 4
    total = keep_ref[...] + give_ref[...].astype(jnp.float32)
    tails = total[4 * half :]
    parts = [(total[slot * half : (slot + 1) * half], tails[2 * slot : 2 * slot + 2]) for slot in range(4)]

    def write(place):
        middle, ends = parts[:2], parts[2:]
        if place in (0, TEAM - 1):
            put(cross_out, middle)
            put(keep_out, (None, ends[0]) if place == 0 else (ends[0], None))
        else:
            put(cross_out, ends if place == 1 else ends[::-1])
            put(keep_out, middle)
        put(side_out, ends[:1])

    for place in range(TEAM):
        pl.when(place_ref[0, 0] == place)(lambda place=place: write(place))


def transform_kernel(place_ref, keep_ref, cross_ref, side_ref, self_out, outer_out):
    members = keep_ref.shape[1]
    half = members // 2
    place = place_ref[0, 0]
    total = keep_ref[...] + cross_ref[...].astype(jnp.float32)
    side = side_ref[...].astype(jnp.float32)
    row = lax.broadcasted_iota(jnp.int32, (half, half), 0)
    col = lax.broadcasted_iota(jnp.int32, (half, half), 1)
    upper = row <= col
    diagonal = row == col
    full_row = lax.broadcasted_iota(jnp.int32, (members, members), 0)
    full_col = lax.broadcasted_iota(jnp.int32, (members, members), 1)
    identity = (full_row == full_col).astype(jnp.float32)

    systems, projections, bounds = [], [], []
    for slot in range(2):
        mine = (place < SIDE) if slot == 0 else (place >= SIDE)
        extra = jnp.where(mine, side, 0.0)
        body = total[slot * half : (slot + 1) * half] + extra[:half]
        tail = total[members + 2 * slot : members + 2 * slot + 2] + extra[half : half + 2]
        mixed = body[:, :half]
        beside = body[:, half:]
        mixed_t = mixed.T
        first = jnp.where(upper, mixed, mixed_t)
        last = jnp.where(diagonal, tail[1:2, :half], jnp.where(upper, mixed_t, mixed))
        gram = jnp.concatenate(
            [jnp.concatenate([first, beside], axis=1), jnp.concatenate([beside.T, last], axis=1)], axis=0
        )
        system = gram + (members - 1.0) * identity
        bound = jnp.max(jnp.sum(jnp.abs(system), axis=0, keepdims=True), axis=1, keepdims=True)
        systems.append(system / bound)
        projections.append(tail[0:1])
        bounds.append(bound)

    current = systems
    factor = [1.5 * identity - 0.5 * x for x in current]
    parts = [split(x) for x in factor]
    roots = parts
    for sweep in range(1, NSI):
        current = [dot3(split(x), f) for x, f in zip(current, parts)]
        factor = [1.5 * identity - 0.5 * dot3(r, split(x)) for r, x in zip(roots, current)]
        parts = [split(x) for x in factor]
        inverse_root = [dot3(f, r) for f, r in zip(parts, roots)]
        roots = [split(x) for x in inverse_root]
    transforms = []
    for root, parts, projection, bound in zip(inverse_root, roots, projections, bounds):
        inner = dot3(split(jnp.broadcast_to(projection, (8, members))), parts)
        centre = dot3(split(inner), parts) / bound
        transforms.append(root * jnp.sqrt((members - 1.0) / bound) + centre.T[:, 0:1])
    even = place % 2 == 0
    self_out[...] = jnp.where(even, transforms[1], transforms[0]).astype(jnp.bfloat16)
    outer_out[...] = jnp.where(even, transforms[0], transforms[1]).astype(jnp.bfloat16)


def other_shares(width):
    return [abs(column - (width - 1) / 2.0) / width for column in range(width)]


def moved_columns(state_ref, columns, transform_ref):
    tile_lat, _, levels, members = state_ref.shape
    rows = state_ref[:, columns].reshape(tile_lat * (columns.stop - columns.start) * levels, members)
    return dot(rows, transform_ref[...]).reshape(tile_lat, -1, levels, members)


def product_kernel(place_ref, self_ref, outer_ref, base_ref, state_ref, out_ref):
    width = state_ref.shape[1]
    half = width // 2
    shares = other_shares(width)
    moved = moved_columns(state_ref, slice(0, width), self_ref)

    def write(outer):
        beside = moved_columns(state_ref, outer, outer_ref)
        for column, other in enumerate(shares):
            value = base_ref[:, column] + (1.0 - other) * moved[:, column]
            if outer.start <= column < outer.stop:
                value = value + other * beside[:, column - outer.start]
            out_ref[:, column] = value

    even = place_ref[0, 0] % 2 == 0

    @pl.when(even)
    def _():
        write(slice(0, half))

    @pl.when(jnp.logical_not(even))
    def _():
        write(slice(half, width))


def blend_kernel(place_ref, inner_ref, part_ref, state_ref, out_ref):
    width = state_ref.shape[1]
    half = width // 2
    shares = other_shares(width)

    def write(inner):
        beside = moved_columns(state_ref, inner, inner_ref)
        for column, other in enumerate(shares):
            value = part_ref[:, column]
            if inner.start <= column < inner.stop:
                value = value + other * beside[:, column - inner.start]
            out_ref[:, column] = value.astype(jnp.bfloat16)

    even = place_ref[0, 0] % 2 == 0

    @pl.when(even)
    def _():
        write(slice(half, width))

    @pl.when(jnp.logical_not(even))
    def _():
        write(slice(0, half))


def shifts(lat_count, lon_count, move):
    pairs = []
    for lat in range(lat_count):
        for lon in range(lon_count):
            target = move(lat, lon)
            if target is not None and 0 <= target[0] < lat_count:
                pairs.append((lat * lon_count + lon, target[0] * lon_count + target[1] % lon_count))
    return pairs


def local(
    anomalies,
    background_mean,
    obs_anom,
    innovation,
    obs_precision,
    obs_blocks,
    localization,
    loc_pattern,
):
    members = obs_anom.shape[2]
    obs_rows = obs_anom.shape[1]
    half = members // 2
    lat_count = lax.axis_size("lat")
    lon_count = lax.axis_size("lon")
    place = (lax.axis_index("lon") % TEAM).astype(jnp.int32).reshape(1, 1)
    bf16, f32 = jnp.bfloat16, jnp.float32

    def call(kernel, outs, ins, *operands, scratch=(), limit=VMEM_LIMIT):
        return pl.pallas_call(
            kernel,
            out_shape=tuple(jax.ShapeDtypeStruct(*out) for out in outs),
            in_specs=ins,
            out_specs=(VMEM,) * len(outs),
            scratch_shapes=scratch,
            compiler_params=pltpu.CompilerParams(vmem_limit_bytes=limit),
            name=kernel.__name__.removesuffix("_kernel"),
        )(*operands)

    def send(value, move):
        return lax.ppermute(value, ("lat", "lon"), shifts(lat_count, lon_count, move))

    def up(lat, lon):
        return lat + 1, lon

    def down(lat, lon):
        return lat - 1, lon

    def other_core(lat, lon):
        return lat, lon ^ 1

    def along_x(lat, lon):
        return lat, lon + (TEAM if lon % TEAM >= SIDE else -TEAM)

    def across_z(lat, lon):
        return lat, lon ^ 2

    def side_move(lat, lon):
        step = {1: TEAM - 1, TEAM - 2: 1 - TEAM}.get(lon % TEAM)
        return None if step is None else (lat, lon + step)

    own, near, far = call(
        prepare_kernel,
        [((members + EXTRA, obs_rows), bf16)] + [((SIDE, EXTRA, obs_rows), bf16)] * 2,
        [SMEM] * 3 + [ANY] * 4,
        place,
        obs_blocks,
        loc_pattern[0],
        obs_anom[0],
        innovation,
        obs_precision,
        localization[0],
        scratch=[
            pltpu.VMEM((obs_rows, members), bf16),
            pltpu.VMEM((1, obs_rows), bf16),
            pltpu.VMEM((1, obs_rows), bf16),
            pltpu.VMEM((1, localization.shape[2]), f32),
            pltpu.VMEM((EXTRA // 2, obs_rows), f32),
            pltpu.SemaphoreType.DMA((4,)),
        ],
        limit=56 * 1024 * 1024,
    )
    cross = send(far, across_z)
    beside = send(own, along_x)
    below = send(own, up)
    above = send(own, down)
    beside_below = send(beside, up)
    beside_above = send(beside, down)
    (core,) = call(
        relay_kernel,
        [((2 * EXTRA + RELAY_ROWS, obs_rows), bf16)],
        [VMEM] * 3,
        near,
        cross,
        beside,
    )
    core = send(core, other_core)

    (shares,) = call(
        early_kernel,
        [((TEAM + 1, members + EXTRA, members), f32)],
        [SMEM] + [VMEM] * 7,
        place,
        near,
        cross,
        core,
        own,
        below,
        above,
        beside,
    )
    give, keep = call(
        late_kernel,
        [((4 * half + EXTRA, members), bf16), ((4 * half + EXTRA, members), f32)],
        [SMEM] + [VMEM] * 6,
        place,
        cross,
        core,
        beside,
        beside_below,
        beside_above,
        shares,
        scratch=[pltpu.VMEM((TEAM + 1, half, members), f32), pltpu.VMEM((TEAM + 1, 8, members), f32)],
    )
    give = send(give, other_core)
    shares, keep, side = call(
        gather_kernel,
        [((members + EXTRA, members), bf16), ((members + EXTRA, members), f32), ((half + EXTRA, members), bf16)],
        [SMEM] + [VMEM] * 2,
        place,
        keep,
        give,
    )
    shares = send(shares, across_z)
    side = send(side, side_move)

    transform, outer = call(
        transform_kernel,
        [((members, members), bf16)] * 2,
        [SMEM] + [VMEM] * 3,
        place,
        keep,
        shares,
        side,
    )
    inner = send(transform, other_core)
    base = jnp.broadcast_to(background_mean[..., None], anomalies.shape)
    (part,) = call(
        product_kernel, [(anomalies.shape, f32)], [SMEM] + [VMEM] * 4, place, transform, outer, base, anomalies
    )
    (analysis,) = call(blend_kernel, [(anomalies.shape, bf16)], [SMEM] + [VMEM] * 3, place, inner, part, anomalies)
    return analysis


def solution(mesh):
    in_specs = (
        P("lat", "lon", None, None),
        P("lat", "lon", None),
        P("lat", "lon", None),
        P("lat", "lon"),
        P("lat", "lon"),
        P("lat", "lon"),
        P("lat", "lon", None),
        P("lat", "lon", None),
    )
    out_specs = P("lat", "lon", None, None)
    return jax.shard_map(local, mesh=mesh, in_specs=in_specs, out_specs=out_specs, check_vma=False)
```

```python
import jax
import jax.numpy as jnp
from jax import lax
from jax.experimental import pallas as pl
from jax.experimental.pallas import tpu as pltpu
from jax.sharding import PartitionSpec as P

LAT_REACH = 1
LON_REACH = 2
NEAR_LAT = 2 * LAT_REACH + 1
NEAR_LON = 2 * LON_REACH + 1
NSI = 5
BLOCK_ROWS = 128
SIDE = 2
TEAM = 4
EXTRA = 16
RELAY_ROWS = 208
VMEM_LIMIT = 32 * 1024 * 1024

ACROSS = (((1,), (1,)), ((), ()))
PLAIN = (((1,), (0,)), ((), ()))
VMEM = pl.BlockSpec(memory_space=pltpu.VMEM)
SMEM = pl.BlockSpec(memory_space=pltpu.SMEM)
ANY = pl.BlockSpec(memory_space=pl.ANY)


def dot(a, b, dims=PLAIN):
    return lax.dot_general(a, b, dims, preferred_element_type=jnp.float32)


def split(x):
    high = x.astype(jnp.bfloat16)
    return high, (x - high.astype(jnp.float32)).astype(jnp.bfloat16)


def dot3(a, b):
    return dot(a[0], b[0]) + (dot(a[0], b[1]) + dot(a[1], b[0]))


def prepare_kernel(
    place_ref,
    blocks_ref,
    pattern_ref,
    anom_hbm,
    innov_hbm,
    prec_hbm,
    local_hbm,
    tile_ref,
    near_ref,
    far_ref,
    anom_ref,
    innov_ref,
    prec_ref,
    local_ref,
    weight_ref,
    sems,
):
    copies = []
    for index, (source, target) in enumerate(
        ((local_hbm, local_ref), (innov_hbm, innov_ref), (prec_hbm, prec_ref), (anom_hbm, anom_ref))
    ):
        copies.append(pltpu.make_async_copy(source, target, sems.at[index]))
        copies[-1].start()
    rows, members = anom_ref.shape
    place = place_ref[0, 0]
    blocks = rows // BLOCK_ROWS
    copies[0].wait()

    def weights(tiles):
        for kind, offset in enumerate(tiles):
            inside = (offset >= -LON_REACH) & (offset <= LON_REACH)
            offset = jnp.clip(offset, -LON_REACH, LON_REACH) + LON_REACH
            for lat in range(NEAR_LAT):
                near = lat * NEAR_LON + offset
                for block in range(blocks):
                    used = jnp.where(inside, pattern_ref[0, near * blocks + block], 0).astype(jnp.float32)
                    start = pl.multiple_of((near * blocks + block) * BLOCK_ROWS, BLOCK_ROWS)
                    weight_ref[pl.ds(kind * NEAR_LAT + lat, 1), pl.ds(block * BLOCK_ROWS, BLOCK_ROWS)] = (
                        local_ref[:, pl.ds(start, BLOCK_ROWS)] * used
                    )
        return weight_ref[...]

    weight_ref[...] = jnp.zeros_like(weight_ref)
    for index in range(TEAM):
        reader = place ^ index
        beside = reader + jnp.where(reader >= SIDE, -TEAM, TEAM)
        pack_ref = near_ref if index < SIDE else far_ref
        pack_ref[index % SIDE] = jnp.concatenate(split(weights((reader - place, beside - place))), axis=0)

    high, low = split(weights((0 * place, 1 - 2 * (place % 2))))
    copies[1].wait()
    copies[2].wait()
    lane = lax.broadcasted_iota(jnp.int32, (1, rows), 1)
    live = (lane < blocks_ref[0, 0] * BLOCK_ROWS).astype(jnp.float32)
    innov = innov_ref[...].astype(jnp.float32)
    prec = prec_ref[...].astype(jnp.float32) * live
    used = 2 * NEAR_LAT
    tail = [innov, prec, high.astype(jnp.float32)[:used], low.astype(jnp.float32)[:used]]
    tail.append(jnp.zeros((EXTRA - 2 - 2 * used, rows), jnp.float32))
    tile_ref[pl.ds(members, EXTRA), :] = jnp.concatenate(tail, axis=0).astype(jnp.bfloat16)
    copies[3].wait()
    tile_ref[pl.ds(0, members), :] = anom_ref[...].T


def joined(pack):
    parts = pack.astype(jnp.float32)
    return parts[: EXTRA // 2] + parts[EXTRA // 2 :]


def relay_kernel(near_ref, cross_ref, beside_ref, out_ref):
    depth = beside_ref.shape[0]
    out_ref[pl.ds(0, EXTRA), :] = near_ref[1]
    out_ref[pl.ds(EXTRA, EXTRA), :] = cross_ref[1]
    out_ref[pl.ds(2 * EXTRA, RELAY_ROWS), :] = beside_ref[pl.ds(depth - RELAY_ROWS, RELAY_ROWS), :]


def outer_weights(place_ref, beside_ref, core_ref):
    members = beside_ref.shape[0] - EXTRA
    place = place_ref[0, 0]
    used = 2 * NEAR_LAT
    direct = beside_ref[pl.ds(members, EXTRA), :].astype(jnp.float32)[2 : 2 + 2 * used]
    passed = core_ref[pl.ds(core_ref.shape[0] - EXTRA, EXTRA), :].astype(jnp.float32)[2 : 2 + 2 * used]
    outer = (place == 0) | (place == TEAM - 1)
    direct = direct[:NEAR_LAT] + direct[used : used + NEAR_LAT]
    passed = passed[NEAR_LAT:used] + passed[used + NEAR_LAT :]
    return jnp.where(outer, direct, passed)


def weighted(tile_ref, weight):
    members = tile_ref.shape[0] - EXTRA
    prec = tile_ref[pl.ds(members, EXTRA), :].astype(jnp.float32)[1:2]
    scaled = (tile_ref[...].astype(jnp.float32) * (weight * prec)).astype(jnp.bfloat16)
    return dot(scaled, tile_ref[pl.ds(0, members), :], ACROSS)


def outer_lats(place_ref, weight):
    below, above = weight[:1], weight[2 * LAT_REACH : 2 * LAT_REACH + 1]
    even = place_ref[0, 0] % 2 == 0
    return jnp.where(even, below, above), jnp.where(even, above, below)


def early_kernel(
    place_ref, near_ref, cross_ref, core_ref, own_ref, first_ref, second_ref, beside_ref, out_ref
):
    for index, pack in enumerate((near_ref[0], core_ref[pl.ds(0, EXTRA), :], cross_ref[0], core_ref[pl.ds(EXTRA, EXTRA), :])):
        weight = joined(pack)
        first, second = outer_lats(place_ref, weight)
        total = weighted(own_ref, weight[LAT_REACH : LAT_REACH + 1])
        total = total + weighted(first_ref, first) + weighted(second_ref, second)
        if index >= SIDE:
            row = NEAR_LAT + LAT_REACH
            total = total + weighted(beside_ref, weight[row : row + 1])
        out_ref[index] = total
    weight = outer_weights(place_ref, beside_ref, core_ref)
    out_ref[TEAM] = weighted(beside_ref, weight[LAT_REACH : LAT_REACH + 1])


def packed(total):
    members = total.shape[1]
    half = members // 2
    row = lax.broadcasted_iota(jnp.int32, (half, half), 0)
    col = lax.broadcasted_iota(jnp.int32, (half, half), 1)
    first = total[:half, :half]
    last = total[half:members, half:]
    diagonal = jnp.sum(jnp.where(row == col, last, 0.0), axis=0, keepdims=True)
    body = jnp.concatenate([jnp.where(row <= col, first, last), total[:half, half:]], axis=1)
    return body, jnp.concatenate(
        [total[members : members + 1], jnp.concatenate([diagonal, diagonal], axis=1)], axis=0
    )


def put(out_ref, parts):
    half, members = next(part[0].shape for part in parts if part is not None)
    tails = []
    for slot, part in enumerate(parts):
        body, tail = part or (jnp.zeros((half, members), jnp.float32), jnp.zeros((2, members), jnp.float32))
        out_ref[pl.ds(slot * half, half), :] = body.astype(out_ref.dtype)
        tails.append(tail)
    tails.append(jnp.zeros((EXTRA - 2 * len(parts), members), jnp.float32))
    out_ref[pl.ds(len(parts) * half, EXTRA), :] = jnp.concatenate(tails, axis=0).astype(out_ref.dtype)


def late_kernel(
    place_ref,
    cross_ref,
    core_ref,
    beside_ref,
    first_ref,
    second_ref,
    share_ref,
    give_ref,
    keep_ref,
    body_ref,
    tail_ref,
):
    for index in range(TEAM + 1):
        total = share_ref[index]
        if index >= SIDE:
            if index < TEAM:
                weight = joined(cross_ref[0] if index == SIDE else core_ref[pl.ds(EXTRA, EXTRA), :])[NEAR_LAT:]
            else:
                weight = outer_weights(place_ref, beside_ref, core_ref)
            first, second = outer_lats(place_ref, weight)
            total = total + weighted(first_ref, first) + weighted(second_ref, second)
        body, tail = packed(total)
        body_ref[index] = body
        tail_ref[index, pl.ds(0, 2), :] = tail

    def write(place):
        def part(index):
            return body_ref[index], tail_ref[index, pl.ds(0, 2), :]

        middle = [part(1 ^ place), part(2 ^ place)]
        if place in (0, TEAM - 1):
            put(give_ref, (*middle, part(3), part(TEAM)))
            put(keep_ref, (*middle, part(0), None))
        else:
            put(give_ref, (*middle, part(1), None))
            put(keep_ref, (*middle, part(2), part(TEAM)))

    for place in range(TEAM):
        pl.when(place_ref[0, 0] == place)(lambda place=place: write(place))


def gather_kernel(place_ref, keep_ref, give_ref, cross_out, keep_out, side_out):
    half = (keep_ref.shape[0] - EXTRA) // 4
    total = keep_ref[...] + give_ref[...].astype(jnp.float32)
    tails = total[4 * half :]
    parts = [(total[slot * half : (slot + 1) * half], tails[2 * slot : 2 * slot + 2]) for slot in range(4)]

    def write(place):
        middle, ends = parts[:2], parts[2:]
        if place in (0, TEAM - 1):
            put(cross_out, middle)
            put(keep_out, (None, ends[0]) if place == 0 else (ends[0], None))
        else:
            put(cross_out, ends if place == 1 else ends[::-1])
            put(keep_out, middle)
        put(side_out, ends[:1])

    for place in range(TEAM):
        pl.when(place_ref[0, 0] == place)(lambda place=place: write(place))


def transform_kernel(place_ref, keep_ref, cross_ref, side_ref, self_out, outer_out):
    members = keep_ref.shape[1]
    half = members // 2
    place = place_ref[0, 0]
    total = keep_ref[...] + cross_ref[...].astype(jnp.float32)
    side = side_ref[...].astype(jnp.float32)
    row = lax.broadcasted_iota(jnp.int32, (half, half), 0)
    col = lax.broadcasted_iota(jnp.int32, (half, half), 1)
    upper = row <= col
    diagonal = row == col
    full_row = lax.broadcasted_iota(jnp.int32, (members, members), 0)
    full_col = lax.broadcasted_iota(jnp.int32, (members, members), 1)
    identity = (full_row == full_col).astype(jnp.float32)

    systems, projections, bounds = [], [], []
    for slot in range(2):
        mine = (place < SIDE) if slot == 0 else (place >= SIDE)
        extra = jnp.where(mine, side, 0.0)
        body = total[slot * half : (slot + 1) * half] + extra[:half]
        tail = total[members + 2 * slot : members + 2 * slot + 2] + extra[half : half + 2]
        mixed = body[:, :half]
        beside = body[:, half:]
        mixed_t = mixed.T
        first = jnp.where(upper, mixed, mixed_t)
        last = jnp.where(diagonal, tail[1:2, :half], jnp.where(upper, mixed_t, mixed))
        gram = jnp.concatenate(
            [jnp.concatenate([first, beside], axis=1), jnp.concatenate([beside.T, last], axis=1)], axis=0
        )
        system = gram + (members - 1.0) * identity
        bound = jnp.max(jnp.sum(jnp.abs(system), axis=0, keepdims=True), axis=1, keepdims=True)
        systems.append(system / bound)
        projections.append(tail[0:1])
        bounds.append(bound)

    current = systems
    factor = [1.5 * identity - 0.5 * x for x in current]
    parts = [split(x) for x in factor]
    roots = parts
    for sweep in range(1, NSI):
        current = [dot3(split(x), f) for x, f in zip(current, parts)]
        factor = [1.5 * identity - 0.5 * dot3(r, split(x)) for r, x in zip(roots, current)]
        parts = [split(x) for x in factor]
        inverse_root = [dot3(f, r) for f, r in zip(parts, roots)]
        roots = [split(x) for x in inverse_root]
    transforms = []
    for root, parts, projection, bound in zip(inverse_root, roots, projections, bounds):
        inner = dot3(split(jnp.broadcast_to(projection, (8, members))), parts)
        centre = dot3(split(inner), parts) / bound
        transforms.append(root * jnp.sqrt((members - 1.0) / bound) + centre.T[:, 0:1])
    even = place % 2 == 0
    self_out[...] = jnp.where(even, transforms[1], transforms[0]).astype(jnp.bfloat16)
    outer_out[...] = jnp.where(even, transforms[0], transforms[1]).astype(jnp.bfloat16)


def other_shares(width):
    return [abs(column - (width - 1) / 2.0) / width for column in range(width)]


def moved_columns(state_ref, columns, transform_ref):
    tile_lat, _, levels, members = state_ref.shape
    rows = state_ref[:, columns].reshape(tile_lat * (columns.stop - columns.start) * levels, members)
    return dot(rows, transform_ref[...]).reshape(tile_lat, -1, levels, members)


def product_kernel(place_ref, self_ref, outer_ref, base_ref, state_ref, out_ref):
    width = state_ref.shape[1]
    half = width // 2
    shares = other_shares(width)
    moved = moved_columns(state_ref, slice(0, width), self_ref)

    def write(outer):
        beside = moved_columns(state_ref, outer, outer_ref)
        for column, other in enumerate(shares):
            value = base_ref[:, column] + (1.0 - other) * moved[:, column]
            if outer.start <= column < outer.stop:
                value = value + other * beside[:, column - outer.start]
            out_ref[:, column] = value

    even = place_ref[0, 0] % 2 == 0

    @pl.when(even)
    def _():
        write(slice(0, half))

    @pl.when(jnp.logical_not(even))
    def _():
        write(slice(half, width))


def blend_kernel(place_ref, inner_ref, part_ref, state_ref, out_ref):
    width = state_ref.shape[1]
    half = width // 2
    shares = other_shares(width)

    def write(inner):
        beside = moved_columns(state_ref, inner, inner_ref)
        for column, other in enumerate(shares):
            value = part_ref[:, column]
            if inner.start <= column < inner.stop:
                value = value + other * beside[:, column - inner.start]
            out_ref[:, column] = value.astype(jnp.bfloat16)

    even = place_ref[0, 0] % 2 == 0

    @pl.when(even)
    def _():
        write(slice(half, width))

    @pl.when(jnp.logical_not(even))
    def _():
        write(slice(0, half))


def shifts(lat_count, lon_count, move):
    pairs = []
    for lat in range(lat_count):
        for lon in range(lon_count):
            target = move(lat, lon)
            if target is not None and 0 <= target[0] < lat_count:
                pairs.append((lat * lon_count + lon, target[0] * lon_count + target[1] % lon_count))
    return pairs


def local(
    anomalies,
    background_mean,
    obs_anom,
    innovation,
    obs_precision,
    obs_blocks,
    localization,
    loc_pattern,
):
    members = obs_anom.shape[2]
    obs_rows = obs_anom.shape[1]
    half = members // 2
    lat_count = lax.axis_size("lat")
    lon_count = lax.axis_size("lon")
    place = (lax.axis_index("lon") % TEAM).astype(jnp.int32).reshape(1, 1)
    bf16, f32 = jnp.bfloat16, jnp.float32

    def call(kernel, outs, ins, *operands, scratch=(), limit=VMEM_LIMIT, pinned=False):
        return pl.pallas_call(
            kernel,
            out_shape=tuple((pltpu.VMEM if pinned else jax.ShapeDtypeStruct)(*out) for out in outs),
            in_specs=ins,
            out_specs=(VMEM,) * len(outs),
            scratch_shapes=scratch,
            compiler_params=pltpu.CompilerParams(vmem_limit_bytes=limit),
            name=kernel.__name__.removesuffix("_kernel"),
        )(*operands)

    def send(value, move):
        return lax.ppermute(value, ("lat", "lon"), shifts(lat_count, lon_count, move))

    def first_move(lat, lon):
        return lat + 1 - 2 * (lon % 2), lon

    def second_move(lat, lon):
        return lat - 1 + 2 * (lon % 2), lon

    def other_core(lat, lon):
        return lat, lon ^ 1

    def along_x(lat, lon):
        return lat, lon + (TEAM if lon % TEAM >= SIDE else -TEAM)

    def across_z(lat, lon):
        return lat, lon ^ 2

    def side_move(lat, lon):
        step = {1: TEAM - 1, TEAM - 2: 1 - TEAM}.get(lon % TEAM)
        return None if step is None else (lat, lon + step)

    own, near, far = call(
        prepare_kernel,
        [((members + EXTRA, obs_rows), bf16)] + [((SIDE, EXTRA, obs_rows), bf16)] * 2,
        [SMEM] * 3 + [ANY] * 4,
        place,
        obs_blocks,
        loc_pattern[0],
        obs_anom[0],
        innovation,
        obs_precision,
        localization[0],
        scratch=[
            pltpu.VMEM((obs_rows, members), bf16),
            pltpu.VMEM((1, obs_rows), bf16),
            pltpu.VMEM((1, obs_rows), bf16),
            pltpu.VMEM((1, localization.shape[2]), f32),
            pltpu.VMEM((EXTRA // 2, obs_rows), f32),
            pltpu.SemaphoreType.DMA((4,)),
        ],
        limit=56 * 1024 * 1024,
        pinned=True,
    )
    cross = send(far, across_z)
    beside = send(own, along_x)
    first = send(own, first_move)
    second = send(own, second_move)
    beside_first = send(beside, first_move)
    beside_second = send(beside, second_move)
    (core,) = call(
        relay_kernel,
        [((2 * EXTRA + RELAY_ROWS, obs_rows), bf16)],
        [VMEM] * 3,
        near,
        cross,
        beside,
    )
    core = send(core, other_core)

    (shares,) = call(
        early_kernel,
        [((TEAM + 1, members + EXTRA, members), f32)],
        [SMEM] + [VMEM] * 7,
        place,
        near,
        cross,
        core,
        own,
        first,
        second,
        beside,
    )
    give, keep = call(
        late_kernel,
        [((4 * half + EXTRA, members), bf16), ((4 * half + EXTRA, members), f32)],
        [SMEM] + [VMEM] * 6,
        place,
        cross,
        core,
        beside,
        beside_first,
        beside_second,
        shares,
        scratch=[pltpu.VMEM((TEAM + 1, half, members), f32), pltpu.VMEM((TEAM + 1, 8, members), f32)],
    )
    give = send(give, other_core)
    shares, keep, side = call(
        gather_kernel,
        [((members + EXTRA, members), bf16), ((members + EXTRA, members), f32), ((half + EXTRA, members), bf16)],
        [SMEM] + [VMEM] * 2,
        place,
        keep,
        give,
    )
    shares = send(shares, across_z)
    side = send(side, side_move)

    transform, outer = call(
        transform_kernel,
        [((members, members), bf16)] * 2,
        [SMEM] + [VMEM] * 3,
        place,
        keep,
        shares,
        side,
    )
    inner = send(transform, other_core)
    base = jnp.broadcast_to(background_mean[..., None], anomalies.shape)
    (part,) = call(
        product_kernel, [(anomalies.shape, f32)], [SMEM] + [VMEM] * 4, place, transform, outer, base, anomalies
    )
    (analysis,) = call(blend_kernel, [(anomalies.shape, bf16)], [SMEM] + [VMEM] * 3, place, inner, part, anomalies)
    return analysis


def solution(mesh):
    in_specs = (
        P("lat", "lon", None, None),
        P("lat", "lon", None),
        P("lat", "lon", None),
        P("lat", "lon"),
        P("lat", "lon"),
        P("lat", "lon"),
        P("lat", "lon", None),
        P("lat", "lon", None),
    )
    out_specs = P("lat", "lon", None, None)
    return jax.shard_map(local, mesh=mesh, in_specs=in_specs, out_specs=out_specs, check_vma=False)
```

```python
import jax
import jax.numpy as jnp
from jax import lax
from jax.experimental import pallas as pl
from jax.experimental.pallas import tpu as pltpu
from jax.sharding import PartitionSpec as P

LAT_REACH = 1
LON_REACH = 2
NEAR_LAT = 2 * LAT_REACH + 1
NEAR_LON = 2 * LON_REACH + 1
NSI = 5
BLOCK_ROWS = 128
SIDE = 2
TEAM = 4
EXTRA = 16
RELAY_ROWS = 208
VMEM_LIMIT = 32 * 1024 * 1024

ACROSS = (((1,), (1,)), ((), ()))
PLAIN = (((1,), (0,)), ((), ()))
VMEM = pl.BlockSpec(memory_space=pltpu.VMEM)
SMEM = pl.BlockSpec(memory_space=pltpu.SMEM)
ANY = pl.BlockSpec(memory_space=pl.ANY)


def dot(a, b, dims=PLAIN):
    return lax.dot_general(a, b, dims, preferred_element_type=jnp.float32)


def split(x):
    high = x.astype(jnp.bfloat16)
    return high, (x - high.astype(jnp.float32)).astype(jnp.bfloat16)


def dot3(a, b):
    return dot(a[0], b[0]) + (dot(a[0], b[1]) + dot(a[1], b[0]))


def prepare_kernel(
    place_ref,
    blocks_ref,
    pattern_ref,
    anom_hbm,
    innov_hbm,
    prec_hbm,
    local_hbm,
    tile_ref,
    near_ref,
    far_ref,
    anom_ref,
    innov_ref,
    prec_ref,
    local_ref,
    weight_ref,
    sems,
):
    copies = []
    for index, (source, target) in enumerate(
        ((local_hbm, local_ref), (innov_hbm, innov_ref), (prec_hbm, prec_ref), (anom_hbm, anom_ref))
    ):
        copies.append(pltpu.make_async_copy(source, target, sems.at[index]))
        copies[-1].start()
    rows, members = anom_ref.shape
    place = place_ref[0, 0]
    blocks = rows // BLOCK_ROWS
    copies[0].wait()

    def weights(tiles):
        for kind, offset in enumerate(tiles):
            inside = (offset >= -LON_REACH) & (offset <= LON_REACH)
            offset = jnp.clip(offset, -LON_REACH, LON_REACH) + LON_REACH
            for lat in range(NEAR_LAT):
                near = lat * NEAR_LON + offset
                for block in range(blocks):
                    used = jnp.where(inside, pattern_ref[0, near * blocks + block], 0).astype(jnp.float32)
                    start = pl.multiple_of((near * blocks + block) * BLOCK_ROWS, BLOCK_ROWS)
                    weight_ref[pl.ds(kind * NEAR_LAT + lat, 1), pl.ds(block * BLOCK_ROWS, BLOCK_ROWS)] = (
                        local_ref[:, pl.ds(start, BLOCK_ROWS)] * used
                    )
        return weight_ref[...]

    weight_ref[...] = jnp.zeros_like(weight_ref)
    for index in range(TEAM):
        reader = place ^ index
        beside = reader + jnp.where(reader >= SIDE, -TEAM, TEAM)
        pack_ref = near_ref if index < SIDE else far_ref
        pack_ref[index % SIDE] = jnp.concatenate(split(weights((reader - place, beside - place))), axis=0)

    high, low = split(weights((0 * place, 1 - 2 * (place % 2))))
    copies[1].wait()
    copies[2].wait()
    lane = lax.broadcasted_iota(jnp.int32, (1, rows), 1)
    live = (lane < blocks_ref[0, 0] * BLOCK_ROWS).astype(jnp.float32)
    innov = innov_ref[...].astype(jnp.float32)
    prec = prec_ref[...].astype(jnp.float32) * live
    used = 2 * NEAR_LAT
    tail = [innov, prec, high.astype(jnp.float32)[:used], low.astype(jnp.float32)[:used]]
    tail.append(jnp.zeros((EXTRA - 2 - 2 * used, rows), jnp.float32))
    tile_ref[pl.ds(members, EXTRA), :] = jnp.concatenate(tail, axis=0).astype(jnp.bfloat16)
    copies[3].wait()
    tile_ref[pl.ds(0, members), :] = anom_ref[...].T


def joined(pack):
    parts = pack.astype(jnp.float32)
    return parts[: EXTRA // 2] + parts[EXTRA // 2 :]


def relay_kernel(near_ref, cross_ref, beside_ref, out_ref):
    depth = beside_ref.shape[0]
    out_ref[pl.ds(0, EXTRA), :] = near_ref[1]
    out_ref[pl.ds(EXTRA, EXTRA), :] = cross_ref[1]
    out_ref[pl.ds(2 * EXTRA, RELAY_ROWS), :] = beside_ref[pl.ds(depth - RELAY_ROWS, RELAY_ROWS), :]


def outer_weights(place_ref, beside_ref, core_ref):
    members = beside_ref.shape[0] - EXTRA
    place = place_ref[0, 0]
    used = 2 * NEAR_LAT
    direct = beside_ref[pl.ds(members, EXTRA), :].astype(jnp.float32)[2 : 2 + 2 * used]
    passed = core_ref[pl.ds(core_ref.shape[0] - EXTRA, EXTRA), :].astype(jnp.float32)[2 : 2 + 2 * used]
    outer = (place == 0) | (place == TEAM - 1)
    direct = direct[:NEAR_LAT] + direct[used : used + NEAR_LAT]
    passed = passed[NEAR_LAT:used] + passed[used + NEAR_LAT :]
    return jnp.where(outer, direct, passed)


def weighted(tile_ref, weight):
    members = tile_ref.shape[0] - EXTRA
    prec = tile_ref[pl.ds(members, EXTRA), :].astype(jnp.float32)[1:2]
    scaled = (tile_ref[...].astype(jnp.float32) * (weight * prec)).astype(jnp.bfloat16)
    return dot(scaled, tile_ref[pl.ds(0, members), :], ACROSS)


def outer_lats(place_ref, weight):
    below, above = weight[:1], weight[2 * LAT_REACH : 2 * LAT_REACH + 1]
    even = place_ref[0, 0] % 2 == 0
    return jnp.where(even, below, above), jnp.where(even, above, below)


def early_kernel(
    place_ref, near_ref, cross_ref, core_ref, own_ref, first_ref, second_ref, beside_ref, out_ref
):
    for index, pack in enumerate((near_ref[0], core_ref[pl.ds(0, EXTRA), :], cross_ref[0], core_ref[pl.ds(EXTRA, EXTRA), :])):
        weight = joined(pack)
        first, second = outer_lats(place_ref, weight)
        total = weighted(own_ref, weight[LAT_REACH : LAT_REACH + 1])
        total = total + weighted(first_ref, first) + weighted(second_ref, second)
        if index >= SIDE:
            row = NEAR_LAT + LAT_REACH
            total = total + weighted(beside_ref, weight[row : row + 1])
        out_ref[index] = total
    weight = outer_weights(place_ref, beside_ref, core_ref)
    out_ref[TEAM] = weighted(beside_ref, weight[LAT_REACH : LAT_REACH + 1])


def packed(total):
    members = total.shape[1]
    half = members // 2
    row = lax.broadcasted_iota(jnp.int32, (half, half), 0)
    col = lax.broadcasted_iota(jnp.int32, (half, half), 1)
    first = total[:half, :half]
    last = total[half:members, half:]
    diagonal = jnp.sum(jnp.where(row == col, last, 0.0), axis=0, keepdims=True)
    body = jnp.concatenate([jnp.where(row <= col, first, last), total[:half, half:]], axis=1)
    return body, jnp.concatenate(
        [total[members : members + 1], jnp.concatenate([diagonal, diagonal], axis=1)], axis=0
    )


def put(out_ref, parts):
    half, members = next(part[0].shape for part in parts if part is not None)
    tails = []
    for slot, part in enumerate(parts):
        body, tail = part or (jnp.zeros((half, members), jnp.float32), jnp.zeros((2, members), jnp.float32))
        out_ref[pl.ds(slot * half, half), :] = body.astype(out_ref.dtype)
        tails.append(tail)
    tails.append(jnp.zeros((EXTRA - 2 * len(parts), members), jnp.float32))
    out_ref[pl.ds(len(parts) * half, EXTRA), :] = jnp.concatenate(tails, axis=0).astype(out_ref.dtype)


def late_kernel(
    place_ref,
    cross_ref,
    core_ref,
    beside_ref,
    first_ref,
    second_ref,
    share_ref,
    give_ref,
    keep_ref,
    body_ref,
    tail_ref,
):
    for index in range(TEAM + 1):
        total = share_ref[index]
        if index >= SIDE:
            if index < TEAM:
                weight = joined(cross_ref[0] if index == SIDE else core_ref[pl.ds(EXTRA, EXTRA), :])[NEAR_LAT:]
            else:
                weight = outer_weights(place_ref, beside_ref, core_ref)
            first, second = outer_lats(place_ref, weight)
            total = total + weighted(first_ref, first) + weighted(second_ref, second)
        body, tail = packed(total)
        body_ref[index] = body
        tail_ref[index, pl.ds(0, 2), :] = tail

    def write(place):
        def part(index):
            return body_ref[index], tail_ref[index, pl.ds(0, 2), :]

        middle = [part(1 ^ place), part(2 ^ place)]
        if place in (0, TEAM - 1):
            put(give_ref, (*middle, part(3), part(TEAM)))
            put(keep_ref, (*middle, part(0), None))
        else:
            put(give_ref, (*middle, part(1), None))
            put(keep_ref, (*middle, part(2), part(TEAM)))

    for place in range(TEAM):
        pl.when(place_ref[0, 0] == place)(lambda place=place: write(place))


def gather_kernel(place_ref, keep_ref, give_ref, cross_out, keep_out, side_out):
    half = (keep_ref.shape[0] - EXTRA) // 4
    total = keep_ref[...] + give_ref[...].astype(jnp.float32)
    tails = total[4 * half :]
    parts = [(total[slot * half : (slot + 1) * half], tails[2 * slot : 2 * slot + 2]) for slot in range(4)]

    def write(place):
        middle, ends = parts[:2], parts[2:]
        if place in (0, TEAM - 1):
            put(cross_out, middle)
            put(keep_out, (None, ends[0]) if place == 0 else (ends[0], None))
        else:
            put(cross_out, ends if place == 1 else ends[::-1])
            put(keep_out, middle)
        put(side_out, ends[:1])

    for place in range(TEAM):
        pl.when(place_ref[0, 0] == place)(lambda place=place: write(place))


def transform_kernel(place_ref, keep_ref, cross_ref, side_ref, self_out, outer_out):
    members = keep_ref.shape[1]
    half = members // 2
    place = place_ref[0, 0]
    total = keep_ref[...] + cross_ref[...].astype(jnp.float32)
    side = side_ref[...].astype(jnp.float32)
    row = lax.broadcasted_iota(jnp.int32, (half, half), 0)
    col = lax.broadcasted_iota(jnp.int32, (half, half), 1)
    upper = row <= col
    diagonal = row == col
    full_row = lax.broadcasted_iota(jnp.int32, (members, members), 0)
    full_col = lax.broadcasted_iota(jnp.int32, (members, members), 1)
    identity = (full_row == full_col).astype(jnp.float32)

    systems, projections, bounds = [], [], []
    for slot in range(2):
        mine = (place < SIDE) if slot == 0 else (place >= SIDE)
        extra = jnp.where(mine, side, 0.0)
        body = total[slot * half : (slot + 1) * half] + extra[:half]
        tail = total[members + 2 * slot : members + 2 * slot + 2] + extra[half : half + 2]
        mixed = body[:, :half]
        beside = body[:, half:]
        mixed_t = mixed.T
        first = jnp.where(upper, mixed, mixed_t)
        last = jnp.where(diagonal, tail[1:2, :half], jnp.where(upper, mixed_t, mixed))
        gram = jnp.concatenate(
            [jnp.concatenate([first, beside], axis=1), jnp.concatenate([beside.T, last], axis=1)], axis=0
        )
        system = gram + (members - 1.0) * identity
        bound = jnp.max(jnp.sum(jnp.abs(system), axis=0, keepdims=True), axis=1, keepdims=True)
        systems.append(system / bound)
        projections.append(jnp.broadcast_to(tail[0:1], (8, members)).T[:, 0:1])
        bounds.append(bound)

    current = systems
    factor = [1.5 * identity - 0.5 * x for x in current]
    parts = [split(x) for x in factor]
    roots = parts
    for sweep in range(1, NSI):
        current = [dot3(split(x), f) for x, f in zip(current, parts)]
        factor = [1.5 * identity - 0.5 * dot3(r, split(x)) for r, x in zip(roots, current)]
        parts = [split(x) for x in factor]
        inverse_root = [dot3(f, r) for f, r in zip(parts, roots)]
        if sweep < NSI - 1:
            roots = [split(x) for x in inverse_root]
    transforms = []
    for root, projection, bound in zip(inverse_root, projections, bounds):
        inner = jnp.sum(root * projection, axis=0, keepdims=True)
        centre = jnp.sum(root * inner, axis=1, keepdims=True) / bound
        transforms.append(root * jnp.sqrt((members - 1.0) / bound) + centre)
    even = place % 2 == 0
    self_out[...] = jnp.where(even, transforms[1], transforms[0]).astype(jnp.bfloat16)
    outer_out[...] = jnp.where(even, transforms[0], transforms[1]).astype(jnp.bfloat16)


def other_shares(width):
    return [abs(column - (width - 1) / 2.0) / width for column in range(width)]


def moved_columns(state_ref, columns, transform_ref):
    tile_lat, _, levels, members = state_ref.shape
    rows = state_ref[:, columns].reshape(tile_lat * (columns.stop - columns.start) * levels, members)
    return dot(rows, transform_ref[...]).reshape(tile_lat, -1, levels, members)


def product_kernel(place_ref, self_ref, outer_ref, base_ref, state_ref, out_ref):
    width = state_ref.shape[1]
    half = width // 2
    shares = other_shares(width)
    moved = moved_columns(state_ref, slice(0, width), self_ref)

    def write(outer):
        beside = moved_columns(state_ref, outer, outer_ref)
        for column, other in enumerate(shares):
            value = base_ref[:, column] + (1.0 - other) * moved[:, column]
            if outer.start <= column < outer.stop:
                value = value + other * beside[:, column - outer.start]
            out_ref[:, column] = value

    even = place_ref[0, 0] % 2 == 0

    @pl.when(even)
    def _():
        write(slice(0, half))

    @pl.when(jnp.logical_not(even))
    def _():
        write(slice(half, width))


def blend_kernel(place_ref, inner_ref, part_ref, state_ref, out_ref):
    width = state_ref.shape[1]
    half = width // 2
    shares = other_shares(width)

    def write(inner):
        beside = moved_columns(state_ref, inner, inner_ref)
        for column, other in enumerate(shares):
            value = part_ref[:, column]
            if inner.start <= column < inner.stop:
                value = value + other * beside[:, column - inner.start]
            out_ref[:, column] = value.astype(jnp.bfloat16)

    even = place_ref[0, 0] % 2 == 0

    @pl.when(even)
    def _():
        write(slice(half, width))

    @pl.when(jnp.logical_not(even))
    def _():
        write(slice(0, half))


def shifts(lat_count, lon_count, move):
    pairs = []
    for lat in range(lat_count):
        for lon in range(lon_count):
            target = move(lat, lon)
            if target is not None and 0 <= target[0] < lat_count:
                pairs.append((lat * lon_count + lon, target[0] * lon_count + target[1] % lon_count))
    return pairs


def local(
    anomalies,
    background_mean,
    obs_anom,
    innovation,
    obs_precision,
    obs_blocks,
    localization,
    loc_pattern,
):
    members = obs_anom.shape[2]
    obs_rows = obs_anom.shape[1]
    half = members // 2
    lat_count = lax.axis_size("lat")
    lon_count = lax.axis_size("lon")
    place = (lax.axis_index("lon") % TEAM).astype(jnp.int32).reshape(1, 1)
    bf16, f32 = jnp.bfloat16, jnp.float32

    def call(kernel, outs, ins, *operands, scratch=(), limit=VMEM_LIMIT, pinned=False):
        return pl.pallas_call(
            kernel,
            out_shape=tuple((pltpu.VMEM if pinned else jax.ShapeDtypeStruct)(*out) for out in outs),
            in_specs=ins,
            out_specs=(VMEM,) * len(outs),
            scratch_shapes=scratch,
            compiler_params=pltpu.CompilerParams(vmem_limit_bytes=limit),
            name=kernel.__name__.removesuffix("_kernel"),
        )(*operands)

    def send(value, move):
        return lax.ppermute(value, ("lat", "lon"), shifts(lat_count, lon_count, move))

    def first_move(lat, lon):
        return lat + 1 - 2 * (lon % 2), lon

    def second_move(lat, lon):
        return lat - 1 + 2 * (lon % 2), lon

    def other_core(lat, lon):
        return lat, lon ^ 1

    def along_x(lat, lon):
        return lat, lon + (TEAM if lon % TEAM >= SIDE else -TEAM)

    def across_z(lat, lon):
        return lat, lon ^ 2

    def side_move(lat, lon):
        step = {1: TEAM - 1, TEAM - 2: 1 - TEAM}.get(lon % TEAM)
        return None if step is None else (lat, lon + step)

    own, near, far = call(
        prepare_kernel,
        [((members + EXTRA, obs_rows), bf16)] + [((SIDE, EXTRA, obs_rows), bf16)] * 2,
        [SMEM] * 3 + [ANY] * 4,
        place,
        obs_blocks,
        loc_pattern[0],
        obs_anom[0],
        innovation,
        obs_precision,
        localization[0],
        scratch=[
            pltpu.VMEM((obs_rows, members), bf16),
            pltpu.VMEM((1, obs_rows), bf16),
            pltpu.VMEM((1, obs_rows), bf16),
            pltpu.VMEM((1, localization.shape[2]), f32),
            pltpu.VMEM((EXTRA // 2, obs_rows), f32),
            pltpu.SemaphoreType.DMA((4,)),
        ],
        limit=56 * 1024 * 1024,
        pinned=True,
    )
    cross = send(far, across_z)
    beside = send(own, along_x)
    first = send(own, first_move)
    second = send(own, second_move)
    beside_first = send(beside, first_move)
    beside_second = send(beside, second_move)
    (core,) = call(
        relay_kernel,
        [((2 * EXTRA + RELAY_ROWS, obs_rows), bf16)],
        [VMEM] * 3,
        near,
        cross,
        beside,
    )
    core = send(core, other_core)

    (shares,) = call(
        early_kernel,
        [((TEAM + 1, members + EXTRA, members), f32)],
        [SMEM] + [VMEM] * 7,
        place,
        near,
        cross,
        core,
        own,
        first,
        second,
        beside,
    )
    give, keep = call(
        late_kernel,
        [((4 * half + EXTRA, members), bf16), ((4 * half + EXTRA, members), f32)],
        [SMEM] + [VMEM] * 6,
        place,
        cross,
        core,
        beside,
        beside_first,
        beside_second,
        shares,
        scratch=[pltpu.VMEM((TEAM + 1, half, members), f32), pltpu.VMEM((TEAM + 1, 8, members), f32)],
    )
    give = send(give, other_core)
    shares, keep, side = call(
        gather_kernel,
        [((members + EXTRA, members), bf16), ((members + EXTRA, members), f32), ((half + EXTRA, members), bf16)],
        [SMEM] + [VMEM] * 2,
        place,
        keep,
        give,
    )
    shares = send(shares, across_z)
    side = send(side, side_move)

    transform, outer = call(
        transform_kernel,
        [((members, members), bf16)] * 2,
        [SMEM] + [VMEM] * 3,
        place,
        keep,
        shares,
        side,
    )
    inner = send(transform, other_core)
    base = jnp.broadcast_to(background_mean[..., None], anomalies.shape)
    (part,) = call(
        product_kernel, [(anomalies.shape, f32)], [SMEM] + [VMEM] * 4, place, transform, outer, base, anomalies
    )
    (analysis,) = call(blend_kernel, [(anomalies.shape, bf16)], [SMEM] + [VMEM] * 3, place, inner, part, anomalies)
    return analysis


def solution(mesh):
    in_specs = (
        P("lat", "lon", None, None),
        P("lat", "lon", None),
        P("lat", "lon", None),
        P("lat", "lon"),
        P("lat", "lon"),
        P("lat", "lon"),
        P("lat", "lon", None),
        P("lat", "lon", None),
    )
    out_specs = P("lat", "lon", None, None)
    return jax.shard_map(local, mesh=mesh, in_specs=in_specs, out_specs=out_specs, check_vma=False)
```

```python
import jax
import jax.numpy as jnp
from jax import lax
from jax.experimental import pallas as pl
from jax.experimental.pallas import tpu as pltpu
from jax.sharding import PartitionSpec as P

LAT_REACH = 1
LON_REACH = 2
NEAR_LAT = 2 * LAT_REACH + 1
NEAR_LON = 2 * LON_REACH + 1
NSI = 5
BLOCK_ROWS = 128
SIDE = 2
TEAM = 4
EXTRA = 16
RELAY_ROWS = 208
VMEM_LIMIT = 32 * 1024 * 1024

ACROSS = (((1,), (1,)), ((), ()))
PLAIN = (((1,), (0,)), ((), ()))
VMEM = pl.BlockSpec(memory_space=pltpu.VMEM)
SMEM = pl.BlockSpec(memory_space=pltpu.SMEM)
ANY = pl.BlockSpec(memory_space=pl.ANY)


def dot(a, b, dims=PLAIN):
    return lax.dot_general(a, b, dims, preferred_element_type=jnp.float32)


def split(x):
    high = x.astype(jnp.bfloat16)
    return high, (x - high.astype(jnp.float32)).astype(jnp.bfloat16)


def dot3(a, b):
    return dot(a[0], b[0]) + (dot(a[0], b[1]) + dot(a[1], b[0]))


def prepare_kernel(
    place_ref,
    blocks_ref,
    pattern_ref,
    anom_hbm,
    innov_hbm,
    prec_hbm,
    local_hbm,
    tile_ref,
    near_ref,
    far_ref,
    anom_ref,
    innov_ref,
    prec_ref,
    local_ref,
    weight_ref,
    sems,
):
    copies = []
    for index, (source, target) in enumerate(
        ((local_hbm, local_ref), (innov_hbm, innov_ref), (prec_hbm, prec_ref), (anom_hbm, anom_ref))
    ):
        copies.append(pltpu.make_async_copy(source, target, sems.at[index]))
        copies[-1].start()
    rows, members = anom_ref.shape
    place = place_ref[0, 0]
    blocks = rows // BLOCK_ROWS
    copies[0].wait()

    def weights(tiles):
        for kind, offset in enumerate(tiles):
            inside = (offset >= -LON_REACH) & (offset <= LON_REACH)
            offset = jnp.clip(offset, -LON_REACH, LON_REACH) + LON_REACH
            for lat in range(NEAR_LAT):
                near = lat * NEAR_LON + offset
                for block in range(blocks):
                    used = jnp.where(inside, pattern_ref[0, near * blocks + block], 0).astype(jnp.float32)
                    start = pl.multiple_of((near * blocks + block) * BLOCK_ROWS, BLOCK_ROWS)
                    weight_ref[pl.ds(kind * NEAR_LAT + lat, 1), pl.ds(block * BLOCK_ROWS, BLOCK_ROWS)] = (
                        local_ref[:, pl.ds(start, BLOCK_ROWS)] * used
                    )
        return weight_ref[...]

    weight_ref[...] = jnp.zeros_like(weight_ref)
    for index in range(TEAM):
        reader = place ^ index
        beside = reader + jnp.where(reader >= SIDE, -TEAM, TEAM)
        pack_ref = near_ref if index < SIDE else far_ref
        pack_ref[index % SIDE] = jnp.concatenate(split(weights((reader - place, beside - place))), axis=0)

    high, low = split(weights((0 * place, 1 - 2 * (place % 2))))
    copies[1].wait()
    copies[2].wait()
    lane = lax.broadcasted_iota(jnp.int32, (1, rows), 1)
    live = (lane < blocks_ref[0, 0] * BLOCK_ROWS).astype(jnp.float32)
    innov = innov_ref[...].astype(jnp.float32)
    prec = prec_ref[...].astype(jnp.float32) * live
    used = 2 * NEAR_LAT
    tail = [innov, prec, high.astype(jnp.float32)[:used], low.astype(jnp.float32)[:used]]
    tail.append(jnp.zeros((EXTRA - 2 - 2 * used, rows), jnp.float32))
    tile_ref[pl.ds(members, EXTRA), :] = jnp.concatenate(tail, axis=0).astype(jnp.bfloat16)
    copies[3].wait()
    tile_ref[pl.ds(0, members), :] = anom_ref[...].T


def joined(pack):
    parts = pack.astype(jnp.float32)
    return parts[: EXTRA // 2] + parts[EXTRA // 2 :]


def relay_kernel(near_ref, cross_ref, beside_ref, out_ref):
    depth = beside_ref.shape[0]
    out_ref[pl.ds(0, EXTRA), :] = near_ref[1]
    out_ref[pl.ds(EXTRA, EXTRA), :] = cross_ref[1]
    out_ref[pl.ds(2 * EXTRA, RELAY_ROWS), :] = beside_ref[pl.ds(depth - RELAY_ROWS, RELAY_ROWS), :]


def outer_weights(place_ref, beside_ref, core_ref):
    members = beside_ref.shape[0] - EXTRA
    place = place_ref[0, 0]
    used = 2 * NEAR_LAT
    direct = beside_ref[pl.ds(members, EXTRA), :].astype(jnp.float32)[2 : 2 + 2 * used]
    passed = core_ref[pl.ds(core_ref.shape[0] - EXTRA, EXTRA), :].astype(jnp.float32)[2 : 2 + 2 * used]
    outer = (place == 0) | (place == TEAM - 1)
    direct = direct[:NEAR_LAT] + direct[used : used + NEAR_LAT]
    passed = passed[NEAR_LAT:used] + passed[used + NEAR_LAT :]
    return jnp.where(outer, direct, passed)


def weighted(tile_ref, weight):
    members = tile_ref.shape[0] - EXTRA
    prec = tile_ref[pl.ds(members, EXTRA), :].astype(jnp.float32)[1:2]
    scaled = (tile_ref[...].astype(jnp.float32) * (weight * prec)).astype(jnp.bfloat16)
    return dot(scaled, tile_ref[pl.ds(0, members), :], ACROSS)


def outer_lats(place_ref, weight):
    below, above = weight[:1], weight[2 * LAT_REACH : 2 * LAT_REACH + 1]
    even = place_ref[0, 0] % 2 == 0
    return jnp.where(even, below, above), jnp.where(even, above, below)


def early_kernel(
    place_ref, near_ref, cross_ref, core_ref, own_ref, first_ref, second_ref, beside_ref, out_ref
):
    for index, pack in enumerate((near_ref[0], core_ref[pl.ds(0, EXTRA), :], cross_ref[0], core_ref[pl.ds(EXTRA, EXTRA), :])):
        weight = joined(pack)
        first, second = outer_lats(place_ref, weight)
        total = weighted(own_ref, weight[LAT_REACH : LAT_REACH + 1])
        total = total + weighted(first_ref, first) + weighted(second_ref, second)
        if index >= SIDE:
            row = NEAR_LAT + LAT_REACH
            total = total + weighted(beside_ref, weight[row : row + 1])
        out_ref[index] = total
    weight = outer_weights(place_ref, beside_ref, core_ref)
    out_ref[TEAM] = weighted(beside_ref, weight[LAT_REACH : LAT_REACH + 1])


def packed(total):
    members = total.shape[1]
    half = members // 2
    row = lax.broadcasted_iota(jnp.int32, (half, half), 0)
    col = lax.broadcasted_iota(jnp.int32, (half, half), 1)
    first = total[:half, :half]
    last = total[half:members, half:]
    diagonal = jnp.sum(jnp.where(row == col, last, 0.0), axis=0, keepdims=True)
    body = jnp.concatenate([jnp.where(row <= col, first, last), total[:half, half:]], axis=1)
    return body, jnp.concatenate(
        [total[members : members + 1], jnp.concatenate([diagonal, diagonal], axis=1)], axis=0
    )


def put(out_ref, parts):
    half, members = next(part[0].shape for part in parts if part is not None)
    tails = []
    for slot, part in enumerate(parts):
        body, tail = part or (jnp.zeros((half, members), jnp.float32), jnp.zeros((2, members), jnp.float32))
        out_ref[pl.ds(slot * half, half), :] = body.astype(out_ref.dtype)
        tails.append(tail)
    tails.append(jnp.zeros((EXTRA - 2 * len(parts), members), jnp.float32))
    out_ref[pl.ds(len(parts) * half, EXTRA), :] = jnp.concatenate(tails, axis=0).astype(out_ref.dtype)


def late_kernel(
    place_ref,
    cross_ref,
    core_ref,
    beside_ref,
    first_ref,
    second_ref,
    share_ref,
    give_ref,
    keep_ref,
    body_ref,
    tail_ref,
):
    for index in range(TEAM + 1):
        total = share_ref[index]
        if index >= SIDE:
            if index < TEAM:
                weight = joined(cross_ref[0] if index == SIDE else core_ref[pl.ds(EXTRA, EXTRA), :])[NEAR_LAT:]
            else:
                weight = outer_weights(place_ref, beside_ref, core_ref)
            first, second = outer_lats(place_ref, weight)
            total = total + weighted(first_ref, first) + weighted(second_ref, second)
        body, tail = packed(total)
        body_ref[index] = body
        tail_ref[index, pl.ds(0, 2), :] = tail

    def write(place):
        def part(index):
            return body_ref[index], tail_ref[index, pl.ds(0, 2), :]

        middle = [part(1 ^ place), part(2 ^ place)]
        if place in (0, TEAM - 1):
            put(give_ref, (*middle, part(3), part(TEAM)))
            put(keep_ref, (*middle, part(0), None))
        else:
            put(give_ref, (*middle, part(1), None))
            put(keep_ref, (*middle, part(2), part(TEAM)))

    for place in range(TEAM):
        pl.when(place_ref[0, 0] == place)(lambda place=place: write(place))


def gather_kernel(place_ref, keep_ref, give_ref, cross_out, keep_out, side_out):
    half = (keep_ref.shape[0] - EXTRA) // 4
    total = keep_ref[...] + give_ref[...].astype(jnp.float32)
    tails = total[4 * half :]
    parts = [(total[slot * half : (slot + 1) * half], tails[2 * slot : 2 * slot + 2]) for slot in range(4)]

    def write(place):
        middle, ends = parts[:2], parts[2:]
        if place in (0, TEAM - 1):
            put(cross_out, middle)
            put(keep_out, (None, ends[0]) if place == 0 else (ends[0], None))
        else:
            put(cross_out, ends if place == 1 else ends[::-1])
            put(keep_out, middle)
        put(side_out, ends[:1])

    for place in range(TEAM):
        pl.when(place_ref[0, 0] == place)(lambda place=place: write(place))


def transform_kernel(place_ref, keep_ref, cross_ref, side_ref, self_out, outer_out):
    members = keep_ref.shape[1]
    half = members // 2
    place = place_ref[0, 0]
    total = keep_ref[...] + cross_ref[...].astype(jnp.float32)
    side = side_ref[...].astype(jnp.float32)
    row = lax.broadcasted_iota(jnp.int32, (half, half), 0)
    col = lax.broadcasted_iota(jnp.int32, (half, half), 1)
    upper = row <= col
    diagonal = row == col
    full_row = lax.broadcasted_iota(jnp.int32, (members, members), 0)
    full_col = lax.broadcasted_iota(jnp.int32, (members, members), 1)
    identity = (full_row == full_col).astype(jnp.float32)

    systems, projections, scales = [], [], []
    for slot in range(2):
        mine = (place < SIDE) if slot == 0 else (place >= SIDE)
        extra = jnp.where(mine, side, 0.0)
        body = total[slot * half : (slot + 1) * half] + extra[:half]
        tail = total[members + 2 * slot : members + 2 * slot + 2] + extra[half : half + 2]
        mixed = body[:, :half]
        beside = body[:, half:]
        mixed_t = mixed.T
        first = jnp.where(upper, mixed, mixed_t)
        last = jnp.where(diagonal, tail[1:2, :half], jnp.where(upper, mixed_t, mixed))
        gram = jnp.concatenate(
            [jnp.concatenate([first, beside], axis=1), jnp.concatenate([beside.T, last], axis=1)], axis=0
        )
        system = gram + (members - 1.0) * identity
        bound = jnp.max(jnp.sum(jnp.abs(system), axis=0, keepdims=True), axis=1, keepdims=True)
        scale = 1.0 / bound
        systems.append(system * scale)
        projections.append(jnp.broadcast_to(tail[0:1], (8, members)).T[:, 0:1])
        scales.append(scale)

    current = systems
    factor = [1.5 * identity - 0.5 * x for x in current]
    parts = [split(x) for x in factor]
    roots = parts
    for sweep in range(1, NSI):
        current = [dot3(split(x), f) for x, f in zip(current, parts)]
        factor = [1.5 * identity - 0.5 * dot3(r, split(x)) for r, x in zip(roots, current)]
        parts = [split(x) for x in factor]
        inverse_root = [dot3(f, r) for f, r in zip(parts, roots)]
        if sweep < NSI - 1:
            roots = [split(x) for x in inverse_root]
    transforms = []
    for root, projection, scale in zip(inverse_root, projections, scales):
        inner = jnp.sum(root * projection, axis=0, keepdims=True)
        centre = jnp.sum(root * inner, axis=1, keepdims=True) * scale
        transforms.append(root * jnp.sqrt((members - 1.0) * scale) + centre)
    even = place % 2 == 0
    self_out[...] = jnp.where(even, transforms[1], transforms[0]).astype(jnp.bfloat16)
    outer_out[...] = jnp.where(even, transforms[0], transforms[1]).astype(jnp.bfloat16)


def other_shares(width):
    return [abs(column - (width - 1) / 2.0) / width for column in range(width)]


def moved_columns(state_ref, columns, transform_ref):
    tile_lat, _, levels, members = state_ref.shape
    rows = state_ref[:, columns].reshape(tile_lat * (columns.stop - columns.start) * levels, members)
    return dot(rows, transform_ref[...]).reshape(tile_lat, -1, levels, members)


def product_kernel(place_ref, self_ref, outer_ref, base_ref, state_ref, out_ref):
    width = state_ref.shape[1]
    half = width // 2
    shares = other_shares(width)
    moved = moved_columns(state_ref, slice(0, width), self_ref)

    def write(outer):
        beside = moved_columns(state_ref, outer, outer_ref)
        for column, other in enumerate(shares):
            value = base_ref[:, column] + (1.0 - other) * moved[:, column]
            if outer.start <= column < outer.stop:
                value = value + other * beside[:, column - outer.start]
            out_ref[:, column] = value

    even = place_ref[0, 0] % 2 == 0

    @pl.when(even)
    def _():
        write(slice(0, half))

    @pl.when(jnp.logical_not(even))
    def _():
        write(slice(half, width))


def blend_kernel(place_ref, inner_ref, part_ref, state_ref, out_ref):
    width = state_ref.shape[1]
    half = width // 2
    shares = other_shares(width)

    def write(inner):
        beside = moved_columns(state_ref, inner, inner_ref)
        for column, other in enumerate(shares):
            value = part_ref[:, column]
            if inner.start <= column < inner.stop:
                value = value + other * beside[:, column - inner.start]
            out_ref[:, column] = value.astype(jnp.bfloat16)

    even = place_ref[0, 0] % 2 == 0

    @pl.when(even)
    def _():
        write(slice(half, width))

    @pl.when(jnp.logical_not(even))
    def _():
        write(slice(0, half))


def shifts(lat_count, lon_count, move):
    pairs = []
    for lat in range(lat_count):
        for lon in range(lon_count):
            target = move(lat, lon)
            if target is not None and 0 <= target[0] < lat_count:
                pairs.append((lat * lon_count + lon, target[0] * lon_count + target[1] % lon_count))
    return pairs


def local(
    anomalies,
    background_mean,
    obs_anom,
    innovation,
    obs_precision,
    obs_blocks,
    localization,
    loc_pattern,
):
    members = obs_anom.shape[2]
    obs_rows = obs_anom.shape[1]
    half = members // 2
    lat_count = lax.axis_size("lat")
    lon_count = lax.axis_size("lon")
    place = (lax.axis_index("lon") % TEAM).astype(jnp.int32).reshape(1, 1)
    bf16, f32 = jnp.bfloat16, jnp.float32

    def call(kernel, outs, ins, *operands, scratch=(), limit=VMEM_LIMIT, pinned=False):
        return pl.pallas_call(
            kernel,
            out_shape=tuple((pltpu.VMEM if pinned else jax.ShapeDtypeStruct)(*out) for out in outs),
            in_specs=ins,
            out_specs=(VMEM,) * len(outs),
            scratch_shapes=scratch,
            compiler_params=pltpu.CompilerParams(vmem_limit_bytes=limit),
            name=kernel.__name__.removesuffix("_kernel"),
        )(*operands)

    def send(value, move):
        return lax.ppermute(value, ("lat", "lon"), shifts(lat_count, lon_count, move))

    def first_move(lat, lon):
        return lat + 1 - 2 * (lon % 2), lon

    def second_move(lat, lon):
        return lat - 1 + 2 * (lon % 2), lon

    def other_core(lat, lon):
        return lat, lon ^ 1

    def along_x(lat, lon):
        return lat, lon + (TEAM if lon % TEAM >= SIDE else -TEAM)

    def across_z(lat, lon):
        return lat, lon ^ 2

    def side_move(lat, lon):
        step = {1: TEAM - 1, TEAM - 2: 1 - TEAM}.get(lon % TEAM)
        return None if step is None else (lat, lon + step)

    own, near, far = call(
        prepare_kernel,
        [((members + EXTRA, obs_rows), bf16)] + [((SIDE, EXTRA, obs_rows), bf16)] * 2,
        [SMEM] * 3 + [ANY] * 4,
        place,
        obs_blocks,
        loc_pattern[0],
        obs_anom[0],
        innovation,
        obs_precision,
        localization[0],
        scratch=[
            pltpu.VMEM((obs_rows, members), bf16),
            pltpu.VMEM((1, obs_rows), bf16),
            pltpu.VMEM((1, obs_rows), bf16),
            pltpu.VMEM((1, localization.shape[2]), f32),
            pltpu.VMEM((EXTRA // 2, obs_rows), f32),
            pltpu.SemaphoreType.DMA((4,)),
        ],
        limit=56 * 1024 * 1024,
        pinned=True,
    )
    cross = send(far, across_z)
    beside = send(own, along_x)
    first = send(own, first_move)
    second = send(own, second_move)
    beside_first = send(beside, first_move)
    beside_second = send(beside, second_move)
    (core,) = call(
        relay_kernel,
        [((2 * EXTRA + RELAY_ROWS, obs_rows), bf16)],
        [VMEM] * 3,
        near,
        cross,
        beside,
    )
    core = send(core, other_core)

    (shares,) = call(
        early_kernel,
        [((TEAM + 1, members + EXTRA, members), f32)],
        [SMEM] + [VMEM] * 7,
        place,
        near,
        cross,
        core,
        own,
        first,
        second,
        beside,
    )
    give, keep = call(
        late_kernel,
        [((4 * half + EXTRA, members), bf16), ((4 * half + EXTRA, members), f32)],
        [SMEM] + [VMEM] * 6,
        place,
        cross,
        core,
        beside,
        beside_first,
        beside_second,
        shares,
        scratch=[pltpu.VMEM((TEAM + 1, half, members), f32), pltpu.VMEM((TEAM + 1, 8, members), f32)],
    )
    give = send(give, other_core)
    shares, keep, side = call(
        gather_kernel,
        [((members + EXTRA, members), bf16), ((members + EXTRA, members), f32), ((half + EXTRA, members), bf16)],
        [SMEM] + [VMEM] * 2,
        place,
        keep,
        give,
    )
    shares = send(shares, across_z)
    side = send(side, side_move)

    transform, outer = call(
        transform_kernel,
        [((members, members), bf16)] * 2,
        [SMEM] + [VMEM] * 3,
        place,
        keep,
        shares,
        side,
    )
    inner = send(transform, other_core)
    base = jnp.broadcast_to(background_mean[..., None], anomalies.shape)
    (part,) = call(
        product_kernel, [(anomalies.shape, f32)], [SMEM] + [VMEM] * 4, place, transform, outer, base, anomalies
    )
    (analysis,) = call(blend_kernel, [(anomalies.shape, bf16)], [SMEM] + [VMEM] * 3, place, inner, part, anomalies)
    return analysis


def solution(mesh):
    in_specs = (
        P("lat", "lon", None, None),
        P("lat", "lon", None),
        P("lat", "lon", None),
        P("lat", "lon"),
        P("lat", "lon"),
        P("lat", "lon"),
        P("lat", "lon", None),
        P("lat", "lon", None),
    )
    out_specs = P("lat", "lon", None, None)
    return jax.shard_map(local, mesh=mesh, in_specs=in_specs, out_specs=out_specs, check_vma=False)
```

```python
import jax
import jax.numpy as jnp
from jax import lax
from jax.experimental import pallas as pl
from jax.experimental.pallas import tpu as pltpu
from jax.sharding import PartitionSpec as P

LAT_REACH = 1
LON_REACH = 2
NEAR_LAT = 2 * LAT_REACH + 1
NEAR_LON = 2 * LON_REACH + 1
NSI = 5
BLOCK_ROWS = 128
SIDE = 2
TEAM = 4
EXTRA = 16
RELAY_ROWS = 160
VMEM_LIMIT = 32 * 1024 * 1024

ACROSS = (((1,), (1,)), ((), ()))
PLAIN = (((1,), (0,)), ((), ()))
VMEM = pl.BlockSpec(memory_space=pltpu.VMEM)
SMEM = pl.BlockSpec(memory_space=pltpu.SMEM)
ANY = pl.BlockSpec(memory_space=pl.ANY)


def dot(a, b, dims=PLAIN):
    return lax.dot_general(a, b, dims, preferred_element_type=jnp.float32)


def split(x):
    high = x.astype(jnp.bfloat16)
    return high, (x - high.astype(jnp.float32)).astype(jnp.bfloat16)


def dot3(a, b):
    return dot(a[0], b[0]) + (dot(a[0], b[1]) + dot(a[1], b[0]))


def prepare_kernel(
    place_ref,
    blocks_ref,
    pattern_ref,
    anom_hbm,
    innov_hbm,
    prec_hbm,
    local_hbm,
    tile_ref,
    near_ref,
    far_ref,
    anom_ref,
    innov_ref,
    prec_ref,
    local_ref,
    weight_ref,
    sems,
):
    copies = []
    for index, (source, target) in enumerate(
        ((local_hbm, local_ref), (innov_hbm, innov_ref), (prec_hbm, prec_ref), (anom_hbm, anom_ref))
    ):
        copies.append(pltpu.make_async_copy(source, target, sems.at[index]))
        copies[-1].start()
    rows, members = anom_ref.shape
    place = place_ref[0, 0]
    blocks = rows // BLOCK_ROWS
    copies[0].wait()

    def weights(tiles):
        for kind, offset in enumerate(tiles):
            inside = (offset >= -LON_REACH) & (offset <= LON_REACH)
            offset = jnp.clip(offset, -LON_REACH, LON_REACH) + LON_REACH
            for lat in range(NEAR_LAT):
                near = lat * NEAR_LON + offset
                for block in range(blocks):
                    used = jnp.where(inside, pattern_ref[0, near * blocks + block], 0).astype(jnp.float32)
                    start = pl.multiple_of((near * blocks + block) * BLOCK_ROWS, BLOCK_ROWS)
                    weight_ref[pl.ds(kind * NEAR_LAT + lat, 1), pl.ds(block * BLOCK_ROWS, BLOCK_ROWS)] = (
                        local_ref[:, pl.ds(start, BLOCK_ROWS)] * used
                    )
        return weight_ref[...]

    weight_ref[...] = jnp.zeros_like(weight_ref)
    for index in range(TEAM):
        reader = place ^ index
        beside = reader + jnp.where(reader >= SIDE, -TEAM, TEAM)
        pack_ref = near_ref if index < SIDE else far_ref
        pack_ref[index % SIDE] = jnp.concatenate(split(weights((reader - place, beside - place))), axis=0)

    high, low = split(weights((0 * place, 1 - 2 * (place % 2))))
    copies[1].wait()
    copies[2].wait()
    lane = lax.broadcasted_iota(jnp.int32, (1, rows), 1)
    live = (lane < blocks_ref[0, 0] * BLOCK_ROWS).astype(jnp.float32)
    innov = innov_ref[...].astype(jnp.float32)
    prec = prec_ref[...].astype(jnp.float32) * live
    used = 2 * NEAR_LAT
    tail = [innov, prec, high.astype(jnp.float32)[:used], low.astype(jnp.float32)[:used]]
    tail.append(jnp.zeros((EXTRA - 2 - 2 * used, rows), jnp.float32))
    tile_ref[pl.ds(members, EXTRA), :] = jnp.concatenate(tail, axis=0).astype(jnp.bfloat16)
    copies[3].wait()
    tile_ref[pl.ds(0, members), :] = anom_ref[...].T


def joined(pack):
    parts = pack.astype(jnp.float32)
    return parts[: EXTRA // 2] + parts[EXTRA // 2 :]


def relay_kernel(near_ref, cross_ref, beside_ref, out_ref):
    depth = beside_ref.shape[0]
    out_ref[pl.ds(0, EXTRA), :] = near_ref[1]
    out_ref[pl.ds(EXTRA, EXTRA), :] = cross_ref[1]
    out_ref[pl.ds(2 * EXTRA, RELAY_ROWS), :] = beside_ref[pl.ds(depth - RELAY_ROWS, RELAY_ROWS), :]


def outer_weights(place_ref, beside_ref, core_ref):
    members = beside_ref.shape[0] - EXTRA
    place = place_ref[0, 0]
    used = 2 * NEAR_LAT
    direct = beside_ref[pl.ds(members, EXTRA), :].astype(jnp.float32)[2 : 2 + 2 * used]
    passed = core_ref[pl.ds(core_ref.shape[0] - EXTRA, EXTRA), :].astype(jnp.float32)[2 : 2 + 2 * used]
    outer = (place == 0) | (place == TEAM - 1)
    direct = direct[:NEAR_LAT] + direct[used : used + NEAR_LAT]
    passed = passed[NEAR_LAT:used] + passed[used + NEAR_LAT :]
    return jnp.where(outer, direct, passed)


def weighted(tile_ref, weight):
    members = tile_ref.shape[0] - EXTRA
    prec = tile_ref[pl.ds(members, EXTRA), :].astype(jnp.float32)[1:2]
    scaled = (tile_ref[...].astype(jnp.float32) * (weight * prec)).astype(jnp.bfloat16)
    return dot(scaled, tile_ref[pl.ds(0, members), :], ACROSS)


def outer_lats(place_ref, weight):
    below, above = weight[:1], weight[2 * LAT_REACH : 2 * LAT_REACH + 1]
    even = place_ref[0, 0] % 2 == 0
    return jnp.where(even, below, above), jnp.where(even, above, below)


def early_kernel(
    place_ref,
    near_ref,
    cross_ref,
    core_ref,
    own_ref,
    first_low_ref,
    first_high_ref,
    second_ref,
    beside_ref,
    out_ref,
    first_ref,
):
    first_ref[...] = first_low_ref[...] + first_high_ref[...]
    for index, pack in enumerate((near_ref[0], core_ref[pl.ds(0, EXTRA), :], cross_ref[0], core_ref[pl.ds(EXTRA, EXTRA), :])):
        weight = joined(pack)
        first, second = outer_lats(place_ref, weight)
        total = weighted(own_ref, weight[LAT_REACH : LAT_REACH + 1])
        total = total + weighted(first_ref, first) + weighted(second_ref, second)
        if index >= SIDE:
            row = NEAR_LAT + LAT_REACH
            total = total + weighted(beside_ref, weight[row : row + 1])
        out_ref[index] = total
    weight = outer_weights(place_ref, beside_ref, core_ref)
    out_ref[TEAM] = weighted(beside_ref, weight[LAT_REACH : LAT_REACH + 1])


def packed(total):
    members = total.shape[1]
    half = members // 2
    row = lax.broadcasted_iota(jnp.int32, (half, half), 0)
    col = lax.broadcasted_iota(jnp.int32, (half, half), 1)
    first = total[:half, :half]
    last = total[half:members, half:]
    diagonal = jnp.sum(jnp.where(row == col, last, 0.0), axis=0, keepdims=True)
    body = jnp.concatenate([jnp.where(row <= col, first, last), total[:half, half:]], axis=1)
    return body, jnp.concatenate(
        [total[members : members + 1], jnp.concatenate([diagonal, diagonal], axis=1)], axis=0
    )


def put(out_ref, parts):
    half, members = next(part[0].shape for part in parts if part is not None)
    tails = []
    for slot, part in enumerate(parts):
        body, tail = part or (jnp.zeros((half, members), jnp.float32), jnp.zeros((2, members), jnp.float32))
        out_ref[pl.ds(slot * half, half), :] = body.astype(out_ref.dtype)
        tails.append(tail)
    tails.append(jnp.zeros((EXTRA - 2 * len(parts), members), jnp.float32))
    out_ref[pl.ds(len(parts) * half, EXTRA), :] = jnp.concatenate(tails, axis=0).astype(out_ref.dtype)


def late_kernel(
    place_ref,
    cross_ref,
    core_ref,
    beside_ref,
    first_ref,
    second_ref,
    share_ref,
    give_ref,
    keep_ref,
    body_ref,
    tail_ref,
):
    for index in range(TEAM + 1):
        total = share_ref[index]
        if index >= SIDE:
            if index < TEAM:
                weight = joined(cross_ref[0] if index == SIDE else core_ref[pl.ds(EXTRA, EXTRA), :])[NEAR_LAT:]
            else:
                weight = outer_weights(place_ref, beside_ref, core_ref)
            first, second = outer_lats(place_ref, weight)
            total = total + weighted(first_ref, first) + weighted(second_ref, second)
        body, tail = packed(total)
        body_ref[index] = body
        tail_ref[index, pl.ds(0, 2), :] = tail

    def write(place):
        def part(index):
            return body_ref[index], tail_ref[index, pl.ds(0, 2), :]

        middle = [part(1 ^ place), part(2 ^ place)]
        if place in (0, TEAM - 1):
            put(give_ref, (*middle, part(3), part(TEAM)))
            put(keep_ref, (*middle, part(0), None))
        else:
            put(give_ref, (*middle, part(1), None))
            put(keep_ref, (*middle, part(2), part(TEAM)))

    for place in range(TEAM):
        pl.when(place_ref[0, 0] == place)(lambda place=place: write(place))


def gather_kernel(place_ref, keep_ref, give_ref, cross_out, keep_out, side_out):
    half = (keep_ref.shape[0] - EXTRA) // 4
    total = keep_ref[...] + give_ref[...].astype(jnp.float32)
    tails = total[4 * half :]
    parts = [(total[slot * half : (slot + 1) * half], tails[2 * slot : 2 * slot + 2]) for slot in range(4)]

    def write(place):
        middle, ends = parts[:2], parts[2:]
        if place in (0, TEAM - 1):
            put(cross_out, middle)
            put(keep_out, (None, ends[0]) if place == 0 else (ends[0], None))
        else:
            put(cross_out, ends if place == 1 else ends[::-1])
            put(keep_out, middle)
        put(side_out, ends[:1])

    for place in range(TEAM):
        pl.when(place_ref[0, 0] == place)(lambda place=place: write(place))


def transform_kernel(place_ref, keep_ref, cross_ref, side_ref, self_out, outer_out):
    members = keep_ref.shape[1]
    half = members // 2
    place = place_ref[0, 0]
    total = keep_ref[...] + cross_ref[...].astype(jnp.float32)
    side = side_ref[...].astype(jnp.float32)
    row = lax.broadcasted_iota(jnp.int32, (half, half), 0)
    col = lax.broadcasted_iota(jnp.int32, (half, half), 1)
    upper = row <= col
    diagonal = row == col
    full_row = lax.broadcasted_iota(jnp.int32, (members, members), 0)
    full_col = lax.broadcasted_iota(jnp.int32, (members, members), 1)
    identity = (full_row == full_col).astype(jnp.float32)

    systems, projections, bounds = [], [], []
    for slot in range(2):
        mine = (place < SIDE) if slot == 0 else (place >= SIDE)
        extra = jnp.where(mine, side, 0.0)
        body = total[slot * half : (slot + 1) * half] + extra[:half]
        tail = total[members + 2 * slot : members + 2 * slot + 2] + extra[half : half + 2]
        mixed = body[:, :half]
        beside = body[:, half:]
        mixed_t = mixed.T
        first = jnp.where(upper, mixed, mixed_t)
        last = jnp.where(diagonal, tail[1:2, :half], jnp.where(upper, mixed_t, mixed))
        gram = jnp.concatenate(
            [jnp.concatenate([first, beside], axis=1), jnp.concatenate([beside.T, last], axis=1)], axis=0
        )
        system = gram + (members - 1.0) * identity
        bound = jnp.max(jnp.sum(jnp.abs(system), axis=0, keepdims=True), axis=1, keepdims=True)
        systems.append(system / bound)
        projections.append(jnp.broadcast_to(tail[0:1], (8, members)).T[:, 0:1])
        bounds.append(bound)

    current = systems
    factor = [1.5 * identity - 0.5 * x for x in current]
    parts = [split(x) for x in factor]
    roots = parts
    for sweep in range(1, NSI):
        current = [dot3(split(x), f) for x, f in zip(current, parts)]
        factor = [1.5 * identity - 0.5 * dot3(r, split(x)) for r, x in zip(roots, current)]
        parts = [split(x) for x in factor]
        inverse_root = [dot3(f, r) for f, r in zip(parts, roots)]
        if sweep < NSI - 1:
            roots = [split(x) for x in inverse_root]
    transforms = []
    for root, projection, bound in zip(inverse_root, projections, bounds):
        inner = jnp.sum(root * projection, axis=0, keepdims=True)
        centre = jnp.sum(root * inner, axis=1, keepdims=True) / bound
        transforms.append(root * jnp.sqrt((members - 1.0) / bound) + centre)
    even = place % 2 == 0
    self_out[...] = jnp.where(even, transforms[1], transforms[0]).astype(jnp.bfloat16)
    outer_out[...] = jnp.where(even, transforms[0], transforms[1]).astype(jnp.bfloat16)


def other_shares(width):
    return [abs(column - (width - 1) / 2.0) / width for column in range(width)]


def moved_columns(state_ref, columns, transform_ref):
    tile_lat, _, levels, members = state_ref.shape
    rows = state_ref[:, columns].reshape(tile_lat * (columns.stop - columns.start) * levels, members)
    return dot(rows, transform_ref[...]).reshape(tile_lat, -1, levels, members)


def product_kernel(place_ref, self_ref, outer_ref, base_ref, state_ref, out_ref):
    width = state_ref.shape[1]
    half = width // 2
    shares = other_shares(width)
    moved = moved_columns(state_ref, slice(0, width), self_ref)

    def write(outer):
        beside = moved_columns(state_ref, outer, outer_ref)
        for column, other in enumerate(shares):
            value = base_ref[:, column] + (1.0 - other) * moved[:, column]
            if outer.start <= column < outer.stop:
                value = value + other * beside[:, column - outer.start]
            out_ref[:, column] = value

    even = place_ref[0, 0] % 2 == 0

    @pl.when(even)
    def _():
        write(slice(0, half))

    @pl.when(jnp.logical_not(even))
    def _():
        write(slice(half, width))


def blend_kernel(place_ref, inner_ref, part_ref, state_ref, out_ref):
    width = state_ref.shape[1]
    half = width // 2
    shares = other_shares(width)

    def write(inner):
        beside = moved_columns(state_ref, inner, inner_ref)
        for column, other in enumerate(shares):
            value = part_ref[:, column]
            if inner.start <= column < inner.stop:
                value = value + other * beside[:, column - inner.start]
            out_ref[:, column] = value.astype(jnp.bfloat16)

    even = place_ref[0, 0] % 2 == 0

    @pl.when(even)
    def _():
        write(slice(half, width))

    @pl.when(jnp.logical_not(even))
    def _():
        write(slice(0, half))


def shifts(lat_count, lon_count, move):
    pairs = []
    for lat in range(lat_count):
        for lon in range(lon_count):
            target = move(lat, lon)
            if target is not None and 0 <= target[0] < lat_count:
                pairs.append((lat * lon_count + lon, target[0] * lon_count + target[1] % lon_count))
    return pairs


def local(
    anomalies,
    background_mean,
    obs_anom,
    innovation,
    obs_precision,
    obs_blocks,
    localization,
    loc_pattern,
):
    members = obs_anom.shape[2]
    obs_rows = obs_anom.shape[1]
    half = members // 2
    lat_count = lax.axis_size("lat")
    lon_count = lax.axis_size("lon")
    place = (lax.axis_index("lon") % TEAM).astype(jnp.int32).reshape(1, 1)
    bf16, f32 = jnp.bfloat16, jnp.float32

    def call(kernel, outs, ins, *operands, scratch=(), limit=VMEM_LIMIT, pinned=False):
        return pl.pallas_call(
            kernel,
            out_shape=tuple((pltpu.VMEM if pinned else jax.ShapeDtypeStruct)(*out) for out in outs),
            in_specs=ins,
            out_specs=(VMEM,) * len(outs),
            scratch_shapes=scratch,
            compiler_params=pltpu.CompilerParams(vmem_limit_bytes=limit),
            name=kernel.__name__.removesuffix("_kernel"),
        )(*operands)

    def send(value, move):
        return lax.ppermute(value, ("lat", "lon"), shifts(lat_count, lon_count, move))

    def first_move(lat, lon):
        return lat + 1 - 2 * (lon % 2), lon

    def second_move(lat, lon):
        return lat - 1 + 2 * (lon % 2), lon

    def other_core(lat, lon):
        return lat, lon ^ 1

    def along_x(lat, lon):
        return lat, lon + (TEAM if lon % TEAM >= SIDE else -TEAM)

    def across_z(lat, lon):
        return lat, lon ^ 2

    def side_move(lat, lon):
        step = {1: TEAM - 1, TEAM - 2: 1 - TEAM}.get(lon % TEAM)
        return None if step is None else (lat, lon + step)

    own, near, far = call(
        prepare_kernel,
        [((members + EXTRA, obs_rows), bf16)] + [((SIDE, EXTRA, obs_rows), bf16)] * 2,
        [SMEM] * 3 + [ANY] * 4,
        place,
        obs_blocks,
        loc_pattern[0],
        obs_anom[0],
        innovation,
        obs_precision,
        localization[0],
        scratch=[
            pltpu.VMEM((obs_rows, members), bf16),
            pltpu.VMEM((1, obs_rows), bf16),
            pltpu.VMEM((1, obs_rows), bf16),
            pltpu.VMEM((1, localization.shape[2]), f32),
            pltpu.VMEM((EXTRA // 2, obs_rows), f32),
            pltpu.SemaphoreType.DMA((4,)),
        ],
        limit=56 * 1024 * 1024,
        pinned=True,
    )
    cross = send(far, across_z)
    beside = send(own, along_x)
    first_low = send(own, lambda lat, lon: first_move(lat, lon) if lon % TEAM < SIDE else None)
    first_high = send(own, lambda lat, lon: first_move(lat, lon) if lon % TEAM >= SIDE else None)
    second = send(own, second_move)
    beside_first = send(beside, first_move)
    beside_second = send(beside, second_move)
    (core,) = call(
        relay_kernel,
        [((2 * EXTRA + RELAY_ROWS, obs_rows), bf16)],
        [VMEM] * 3,
        near,
        cross,
        beside,
    )
    core = send(core, other_core)

    (shares,) = call(
        early_kernel,
        [((TEAM + 1, members + EXTRA, members), f32)],
        [SMEM] + [VMEM] * 8,
        place,
        near,
        cross,
        core,
        own,
        first_low,
        first_high,
        second,
        beside,
        scratch=[pltpu.VMEM((members + EXTRA, obs_rows), bf16)],
    )
    give, keep = call(
        late_kernel,
        [((4 * half + EXTRA, members), bf16), ((4 * half + EXTRA, members), f32)],
        [SMEM] + [VMEM] * 6,
        place,
        cross,
        core,
        beside,
        beside_first,
        beside_second,
        shares,
        scratch=[pltpu.VMEM((TEAM + 1, half, members), f32), pltpu.VMEM((TEAM + 1, 8, members), f32)],
    )
    give = send(give, other_core)
    shares, keep, side = call(
        gather_kernel,
        [((members + EXTRA, members), bf16), ((members + EXTRA, members), f32), ((half + EXTRA, members), bf16)],
        [SMEM] + [VMEM] * 2,
        place,
        keep,
        give,
    )
    shares = send(shares, across_z)
    side = send(side, side_move)

    transform, outer = call(
        transform_kernel,
        [((members, members), bf16)] * 2,
        [SMEM] + [VMEM] * 3,
        place,
        keep,
        shares,
        side,
    )
    inner = send(transform, other_core)
    base = jnp.broadcast_to(background_mean[..., None], anomalies.shape)
    (part,) = call(
        product_kernel, [(anomalies.shape, f32)], [SMEM] + [VMEM] * 4, place, transform, outer, base, anomalies
    )
    (analysis,) = call(blend_kernel, [(anomalies.shape, bf16)], [SMEM] + [VMEM] * 3, place, inner, part, anomalies)
    return analysis


def solution(mesh):
    in_specs = (
        P("lat", "lon", None, None),
        P("lat", "lon", None),
        P("lat", "lon", None),
        P("lat", "lon"),
        P("lat", "lon"),
        P("lat", "lon"),
        P("lat", "lon", None),
        P("lat", "lon", None),
    )
    out_specs = P("lat", "lon", None, None)
    return jax.shard_map(local, mesh=mesh, in_specs=in_specs, out_specs=out_specs, check_vma=False)
```

```python
import jax
import jax.numpy as jnp
from jax import lax
from jax.experimental import pallas as pl
from jax.experimental.pallas import tpu as pltpu
from jax.sharding import PartitionSpec as P

LAT_REACH = 1
LON_REACH = 2
NEAR_LAT = 2 * LAT_REACH + 1
NEAR_LON = 2 * LON_REACH + 1
NSI = 5
BLOCK_ROWS = 128
SIDE = 2
TEAM = 4
EXTRA = 16
RELAY_ROWS = 208
VMEM_LIMIT = 32 * 1024 * 1024

ACROSS = (((1,), (1,)), ((), ()))
PLAIN = (((1,), (0,)), ((), ()))
VMEM = pl.BlockSpec(memory_space=pltpu.VMEM)
SMEM = pl.BlockSpec(memory_space=pltpu.SMEM)
ANY = pl.BlockSpec(memory_space=pl.ANY)


def dot(a, b, dims=PLAIN):
    return lax.dot_general(a, b, dims, preferred_element_type=jnp.float32)


def split(x):
    high = x.astype(jnp.bfloat16)
    return high, (x - high.astype(jnp.float32)).astype(jnp.bfloat16)


def dot3(a, b):
    return dot(a[0], b[0]) + (dot(a[0], b[1]) + dot(a[1], b[0]))


def prepare_kernel(
    place_ref,
    blocks_ref,
    pattern_ref,
    anom_hbm,
    innov_hbm,
    prec_hbm,
    local_hbm,
    tile_ref,
    near_ref,
    far_ref,
    anom_ref,
    innov_ref,
    prec_ref,
    local_ref,
    weight_ref,
    sems,
):
    copies = []
    for index, (source, target) in enumerate(
        ((local_hbm, local_ref), (innov_hbm, innov_ref), (prec_hbm, prec_ref), (anom_hbm, anom_ref))
    ):
        copies.append(pltpu.make_async_copy(source, target, sems.at[index]))
    for index in (3, 0, 1, 2):
        copies[index].start()
    rows, members = anom_ref.shape
    place = place_ref[0, 0]
    blocks = rows // BLOCK_ROWS
    copies[0].wait()

    def weights(tiles):
        for kind, offset in enumerate(tiles):
            inside = (offset >= -LON_REACH) & (offset <= LON_REACH)
            offset = jnp.clip(offset, -LON_REACH, LON_REACH) + LON_REACH
            for lat in range(NEAR_LAT):
                near = lat * NEAR_LON + offset
                for block in range(blocks):
                    used = jnp.where(inside, pattern_ref[0, near * blocks + block], 0).astype(jnp.float32)
                    start = pl.multiple_of((near * blocks + block) * BLOCK_ROWS, BLOCK_ROWS)
                    weight_ref[pl.ds(kind * NEAR_LAT + lat, 1), pl.ds(block * BLOCK_ROWS, BLOCK_ROWS)] = (
                        local_ref[:, pl.ds(start, BLOCK_ROWS)] * used
                    )
        return weight_ref[...]

    weight_ref[...] = jnp.zeros_like(weight_ref)
    for index in range(TEAM):
        reader = place ^ index
        beside = reader + jnp.where(reader >= SIDE, -TEAM, TEAM)
        pack_ref = near_ref if index < SIDE else far_ref
        pack_ref[index % SIDE] = jnp.concatenate(split(weights((reader - place, beside - place))), axis=0)

    high, low = split(weights((0 * place, 1 - 2 * (place % 2))))
    copies[1].wait()
    copies[2].wait()
    lane = lax.broadcasted_iota(jnp.int32, (1, rows), 1)
    live = (lane < blocks_ref[0, 0] * BLOCK_ROWS).astype(jnp.float32)
    innov = innov_ref[...].astype(jnp.float32)
    prec = prec_ref[...].astype(jnp.float32) * live
    used = 2 * NEAR_LAT
    tail = [innov, prec, high.astype(jnp.float32)[:used], low.astype(jnp.float32)[:used]]
    tail.append(jnp.zeros((EXTRA - 2 - 2 * used, rows), jnp.float32))
    tile_ref[pl.ds(members, EXTRA), :] = jnp.concatenate(tail, axis=0).astype(jnp.bfloat16)
    copies[3].wait()
    tile_ref[pl.ds(0, members), :] = anom_ref[...].T


def joined(pack):
    parts = pack.astype(jnp.float32)
    return parts[: EXTRA // 2] + parts[EXTRA // 2 :]


def relay_kernel(near_ref, cross_ref, beside_ref, out_ref):
    depth = beside_ref.shape[0]
    out_ref[pl.ds(0, EXTRA), :] = near_ref[1]
    out_ref[pl.ds(EXTRA, EXTRA), :] = cross_ref[1]
    out_ref[pl.ds(2 * EXTRA, RELAY_ROWS), :] = beside_ref[pl.ds(depth - RELAY_ROWS, RELAY_ROWS), :]


def outer_weights(place_ref, beside_ref, core_ref):
    members = beside_ref.shape[0] - EXTRA
    place = place_ref[0, 0]
    used = 2 * NEAR_LAT
    direct = beside_ref[pl.ds(members, EXTRA), :].astype(jnp.float32)[2 : 2 + 2 * used]
    passed = core_ref[pl.ds(core_ref.shape[0] - EXTRA, EXTRA), :].astype(jnp.float32)[2 : 2 + 2 * used]
    outer = (place == 0) | (place == TEAM - 1)
    direct = direct[:NEAR_LAT] + direct[used : used + NEAR_LAT]
    passed = passed[NEAR_LAT:used] + passed[used + NEAR_LAT :]
    return jnp.where(outer, direct, passed)


def weighted(tile_ref, weight):
    members = tile_ref.shape[0] - EXTRA
    prec = tile_ref[pl.ds(members, EXTRA), :].astype(jnp.float32)[1:2]
    scaled = (tile_ref[...].astype(jnp.float32) * (weight * prec)).astype(jnp.bfloat16)
    return dot(scaled, tile_ref[pl.ds(0, members), :], ACROSS)


def outer_lats(place_ref, weight):
    below, above = weight[:1], weight[2 * LAT_REACH : 2 * LAT_REACH + 1]
    even = place_ref[0, 0] % 2 == 0
    return jnp.where(even, below, above), jnp.where(even, above, below)


def early_kernel(
    place_ref, near_ref, cross_ref, core_ref, own_ref, first_ref, second_ref, beside_ref, out_ref
):
    for index, pack in enumerate((near_ref[0], core_ref[pl.ds(0, EXTRA), :], cross_ref[0], core_ref[pl.ds(EXTRA, EXTRA), :])):
        weight = joined(pack)
        first, second = outer_lats(place_ref, weight)
        total = weighted(own_ref, weight[LAT_REACH : LAT_REACH + 1])
        total = total + weighted(first_ref, first) + weighted(second_ref, second)
        if index >= SIDE:
            row = NEAR_LAT + LAT_REACH
            total = total + weighted(beside_ref, weight[row : row + 1])
        out_ref[index] = total
    weight = outer_weights(place_ref, beside_ref, core_ref)
    out_ref[TEAM] = weighted(beside_ref, weight[LAT_REACH : LAT_REACH + 1])


def packed(total):
    members = total.shape[1]
    half = members // 2
    row = lax.broadcasted_iota(jnp.int32, (half, half), 0)
    col = lax.broadcasted_iota(jnp.int32, (half, half), 1)
    first = total[:half, :half]
    last = total[half:members, half:]
    diagonal = jnp.sum(jnp.where(row == col, last, 0.0), axis=0, keepdims=True)
    body = jnp.concatenate([jnp.where(row <= col, first, last), total[:half, half:]], axis=1)
    return body, jnp.concatenate(
        [total[members : members + 1], jnp.concatenate([diagonal, diagonal], axis=1)], axis=0
    )


def put(out_ref, parts):
    half, members = next(part[0].shape for part in parts if part is not None)
    tails = []
    for slot, part in enumerate(parts):
        body, tail = part or (jnp.zeros((half, members), jnp.float32), jnp.zeros((2, members), jnp.float32))
        out_ref[pl.ds(slot * half, half), :] = body.astype(out_ref.dtype)
        tails.append(tail)
    tails.append(jnp.zeros((EXTRA - 2 * len(parts), members), jnp.float32))
    out_ref[pl.ds(len(parts) * half, EXTRA), :] = jnp.concatenate(tails, axis=0).astype(out_ref.dtype)


def late_kernel(
    place_ref,
    cross_ref,
    core_ref,
    beside_ref,
    first_ref,
    second_ref,
    share_ref,
    give_ref,
    keep_ref,
    body_ref,
    tail_ref,
):
    for index in range(TEAM + 1):
        total = share_ref[index]
        if index >= SIDE:
            if index < TEAM:
                weight = joined(cross_ref[0] if index == SIDE else core_ref[pl.ds(EXTRA, EXTRA), :])[NEAR_LAT:]
            else:
                weight = outer_weights(place_ref, beside_ref, core_ref)
            first, second = outer_lats(place_ref, weight)
            total = total + weighted(first_ref, first) + weighted(second_ref, second)
        body, tail = packed(total)
        body_ref[index] = body
        tail_ref[index, pl.ds(0, 2), :] = tail

    def write(place):
        def part(index):
            return body_ref[index], tail_ref[index, pl.ds(0, 2), :]

        middle = [part(1 ^ place), part(2 ^ place)]
        if place in (0, TEAM - 1):
            put(give_ref, (*middle, part(3), part(TEAM)))
            put(keep_ref, (*middle, part(0), None))
        else:
            put(give_ref, (*middle, part(1), None))
            put(keep_ref, (*middle, part(2), part(TEAM)))

    for place in range(TEAM):
        pl.when(place_ref[0, 0] == place)(lambda place=place: write(place))


def gather_kernel(place_ref, keep_ref, give_ref, cross_out, keep_out, side_out):
    half = (keep_ref.shape[0] - EXTRA) // 4
    total = keep_ref[...] + give_ref[...].astype(jnp.float32)
    tails = total[4 * half :]
    parts = [(total[slot * half : (slot + 1) * half], tails[2 * slot : 2 * slot + 2]) for slot in range(4)]

    def write(place):
        middle, ends = parts[:2], parts[2:]
        if place in (0, TEAM - 1):
            put(cross_out, middle)
            put(keep_out, (None, ends[0]) if place == 0 else (ends[0], None))
        else:
            put(cross_out, ends if place == 1 else ends[::-1])
            put(keep_out, middle)
        put(side_out, ends[:1])

    for place in range(TEAM):
        pl.when(place_ref[0, 0] == place)(lambda place=place: write(place))


def transform_kernel(place_ref, keep_ref, cross_ref, side_ref, self_out, outer_out):
    members = keep_ref.shape[1]
    half = members // 2
    place = place_ref[0, 0]
    total = keep_ref[...] + cross_ref[...].astype(jnp.float32)
    side = side_ref[...].astype(jnp.float32)
    row = lax.broadcasted_iota(jnp.int32, (half, half), 0)
    col = lax.broadcasted_iota(jnp.int32, (half, half), 1)
    upper = row <= col
    diagonal = row == col
    full_row = lax.broadcasted_iota(jnp.int32, (members, members), 0)
    full_col = lax.broadcasted_iota(jnp.int32, (members, members), 1)
    identity = (full_row == full_col).astype(jnp.float32)

    systems, projections, bounds = [], [], []
    for slot in range(2):
        mine = (place < SIDE) if slot == 0 else (place >= SIDE)
        extra = jnp.where(mine, side, 0.0)
        body = total[slot * half : (slot + 1) * half] + extra[:half]
        tail = total[members + 2 * slot : members + 2 * slot + 2] + extra[half : half + 2]
        mixed = body[:, :half]
        beside = body[:, half:]
        mixed_t = mixed.T
        first = jnp.where(upper, mixed, mixed_t)
        last = jnp.where(diagonal, tail[1:2, :half], jnp.where(upper, mixed_t, mixed))
        gram = jnp.concatenate(
            [jnp.concatenate([first, beside], axis=1), jnp.concatenate([beside.T, last], axis=1)], axis=0
        )
        system = gram + (members - 1.0) * identity
        bound = jnp.max(jnp.sum(jnp.abs(system), axis=0, keepdims=True), axis=1, keepdims=True)
        systems.append(system / bound)
        projections.append(jnp.broadcast_to(tail[0:1], (8, members)).T[:, 0:1])
        bounds.append(bound)

    current = systems
    factor = [1.5 * identity - 0.5 * x for x in current]
    parts = [split(x) for x in factor]
    roots = parts
    for sweep in range(1, NSI):
        current = [dot3(split(x), f) for x, f in zip(current, parts)]
        factor = [1.5 * identity - 0.5 * dot3(r, split(x)) for r, x in zip(roots, current)]
        parts = [split(x) for x in factor]
        inverse_root = [dot3(f, r) for f, r in zip(parts, roots)]
        if sweep < NSI - 1:
            roots = [split(x) for x in inverse_root]
    transforms = []
    for root, projection, bound in zip(inverse_root, projections, bounds):
        inner = jnp.sum(root * projection, axis=0, keepdims=True)
        centre = jnp.sum(root * inner, axis=1, keepdims=True) / bound
        transforms.append(root * jnp.sqrt((members - 1.0) / bound) + centre)
    even = place % 2 == 0
    self_out[...] = jnp.where(even, transforms[1], transforms[0]).astype(jnp.bfloat16)
    outer_out[...] = jnp.where(even, transforms[0], transforms[1]).astype(jnp.bfloat16)


def other_shares(width):
    return [abs(column - (width - 1) / 2.0) / width for column in range(width)]


def moved_columns(state_ref, columns, transform_ref):
    tile_lat, _, levels, members = state_ref.shape
    rows = state_ref[:, columns].reshape(tile_lat * (columns.stop - columns.start) * levels, members)
    return dot(rows, transform_ref[...]).reshape(tile_lat, -1, levels, members)


def product_kernel(place_ref, self_ref, outer_ref, base_ref, state_ref, out_ref):
    width = state_ref.shape[1]
    half = width // 2
    shares = other_shares(width)
    moved = moved_columns(state_ref, slice(0, width), self_ref)

    def write(outer):
        beside = moved_columns(state_ref, outer, outer_ref)
        for column, other in enumerate(shares):
            value = base_ref[:, column] + (1.0 - other) * moved[:, column]
            if outer.start <= column < outer.stop:
                value = value + other * beside[:, column - outer.start]
            out_ref[:, column] = value

    even = place_ref[0, 0] % 2 == 0

    @pl.when(even)
    def _():
        write(slice(0, half))

    @pl.when(jnp.logical_not(even))
    def _():
        write(slice(half, width))


def blend_kernel(place_ref, inner_ref, part_ref, state_ref, out_ref):
    width = state_ref.shape[1]
    half = width // 2
    shares = other_shares(width)

    def write(inner):
        beside = moved_columns(state_ref, inner, inner_ref)
        for column, other in enumerate(shares):
            value = part_ref[:, column]
            if inner.start <= column < inner.stop:
                value = value + other * beside[:, column - inner.start]
            out_ref[:, column] = value.astype(jnp.bfloat16)

    even = place_ref[0, 0] % 2 == 0

    @pl.when(even)
    def _():
        write(slice(half, width))

    @pl.when(jnp.logical_not(even))
    def _():
        write(slice(0, half))


def shifts(lat_count, lon_count, move):
    pairs = []
    for lat in range(lat_count):
        for lon in range(lon_count):
            target = move(lat, lon)
            if target is not None and 0 <= target[0] < lat_count:
                pairs.append((lat * lon_count + lon, target[0] * lon_count + target[1] % lon_count))
    return pairs


def local(
    anomalies,
    background_mean,
    obs_anom,
    innovation,
    obs_precision,
    obs_blocks,
    localization,
    loc_pattern,
):
    members = obs_anom.shape[2]
    obs_rows = obs_anom.shape[1]
    half = members // 2
    lat_count = lax.axis_size("lat")
    lon_count = lax.axis_size("lon")
    place = (lax.axis_index("lon") % TEAM).astype(jnp.int32).reshape(1, 1)
    bf16, f32 = jnp.bfloat16, jnp.float32

    def call(kernel, outs, ins, *operands, scratch=(), limit=VMEM_LIMIT, pinned=False):
        return pl.pallas_call(
            kernel,
            out_shape=tuple((pltpu.VMEM if pinned else jax.ShapeDtypeStruct)(*out) for out in outs),
            in_specs=ins,
            out_specs=(VMEM,) * len(outs),
            scratch_shapes=scratch,
            compiler_params=pltpu.CompilerParams(vmem_limit_bytes=limit),
            name=kernel.__name__.removesuffix("_kernel"),
        )(*operands)

    def send(value, move):
        return lax.ppermute(value, ("lat", "lon"), shifts(lat_count, lon_count, move))

    def first_move(lat, lon):
        return lat + 1 - 2 * (lon % 2), lon

    def second_move(lat, lon):
        return lat - 1 + 2 * (lon % 2), lon

    def other_core(lat, lon):
        return lat, lon ^ 1

    def along_x(lat, lon):
        return lat, lon + (TEAM if lon % TEAM >= SIDE else -TEAM)

    def across_z(lat, lon):
        return lat, lon ^ 2

    def side_move(lat, lon):
        step = {1: TEAM - 1, TEAM - 2: 1 - TEAM}.get(lon % TEAM)
        return None if step is None else (lat, lon + step)

    own, near, far = call(
        prepare_kernel,
        [((members + EXTRA, obs_rows), bf16)] + [((SIDE, EXTRA, obs_rows), bf16)] * 2,
        [SMEM] * 3 + [ANY] * 4,
        place,
        obs_blocks,
        loc_pattern[0],
        obs_anom[0],
        innovation,
        obs_precision,
        localization[0],
        scratch=[
            pltpu.VMEM((obs_rows, members), bf16),
            pltpu.VMEM((1, obs_rows), bf16),
            pltpu.VMEM((1, obs_rows), bf16),
            pltpu.VMEM((1, localization.shape[2]), f32),
            pltpu.VMEM((EXTRA // 2, obs_rows), f32),
            pltpu.SemaphoreType.DMA((4,)),
        ],
        limit=56 * 1024 * 1024,
        pinned=True,
    )
    cross = send(far, across_z)
    beside = send(own, along_x)
    first = send(own, first_move)
    second = send(own, second_move)
    beside_first = send(beside, first_move)
    beside_second = send(beside, second_move)
    (core,) = call(
        relay_kernel,
        [((2 * EXTRA + RELAY_ROWS, obs_rows), bf16)],
        [VMEM] * 3,
        near,
        cross,
        beside,
    )
    core = send(core, other_core)

    (shares,) = call(
        early_kernel,
        [((TEAM + 1, members + EXTRA, members), f32)],
        [SMEM] + [VMEM] * 7,
        place,
        near,
        cross,
        core,
        own,
        first,
        second,
        beside,
    )
    give, keep = call(
        late_kernel,
        [((4 * half + EXTRA, members), bf16), ((4 * half + EXTRA, members), f32)],
        [SMEM] + [VMEM] * 6,
        place,
        cross,
        core,
        beside,
        beside_first,
        beside_second,
        shares,
        scratch=[pltpu.VMEM((TEAM + 1, half, members), f32), pltpu.VMEM((TEAM + 1, 8, members), f32)],
    )
    give = send(give, other_core)
    shares, keep, side = call(
        gather_kernel,
        [((members + EXTRA, members), bf16), ((members + EXTRA, members), f32), ((half + EXTRA, members), bf16)],
        [SMEM] + [VMEM] * 2,
        place,
        keep,
        give,
    )
    shares = send(shares, across_z)
    side = send(side, side_move)

    transform, outer = call(
        transform_kernel,
        [((members, members), bf16)] * 2,
        [SMEM] + [VMEM] * 3,
        place,
        keep,
        shares,
        side,
    )
    inner = send(transform, other_core)
    base = jnp.broadcast_to(background_mean[..., None], anomalies.shape)
    (part,) = call(
        product_kernel, [(anomalies.shape, f32)], [SMEM] + [VMEM] * 4, place, transform, outer, base, anomalies
    )
    (analysis,) = call(blend_kernel, [(anomalies.shape, bf16)], [SMEM] + [VMEM] * 3, place, inner, part, anomalies)
    return analysis


def solution(mesh):
    in_specs = (
        P("lat", "lon", None, None),
        P("lat", "lon", None),
        P("lat", "lon", None),
        P("lat", "lon"),
        P("lat", "lon"),
        P("lat", "lon"),
        P("lat", "lon", None),
        P("lat", "lon", None),
    )
    out_specs = P("lat", "lon", None, None)
    return jax.shard_map(local, mesh=mesh, in_specs=in_specs, out_specs=out_specs, check_vma=False)
```
